512 devices in a mesh: row: 32 (over z, y_hi), col: 16 (over y_lo, x, core).
Axes of the slice: x: 4, y: 8 (y_hi: 4, y_lo: 2; y = y_hi * 2 + y_lo), z: 8, core: 2. Of those that a mesh axis runs over, the one named last changes fastest.
Arguments:
- pair: bfloat16 [256, 2048, 128], P('row', 'col'), may hold values from -6 to 6
- panel_left: bfloat16 [256, 2048, 128], P('row', 'col'), may hold values from -6 to 6
- panel_right: bfloat16 [2048, 2048, 128], P('row', 'col'), may hold values from -6 to 6
- single: bfloat16 [2048, 384], P('row'), may hold values from -6 to 6
- token_mask: int32 [2048], P('row'), may hold values from 0 to 1, as said below
- chain_ids: int32 [2048], P('row'), may hold values from 0 to 3, never falling along the last dimension, each value on 1 to 1024 neighbouring positions
- w_tri_gate: bfloat16 [128, 128], replicated, may hold values from -0.5 to 0.5
- w_tri_out: bfloat16 [128, 128], replicated, may hold values from -0.5 to 0.5
- w_trans_in: bfloat16 [128, 1024], replicated, may hold values from -0.5 to 0.5
- w_trans_down: bfloat16 [512, 128], replicated, may hold values from -0.25 to 0.25
- w_bias: bfloat16 [128, 16], replicated, may hold values from -1.5 to 1.5
- chain_bias: float32 [16], replicated, may hold values from -2 to 2
- w_attn: bfloat16 [4, 384, 384], P(None, None, 'col'), may hold values from -0.3125 to 0.3125
- w_attn_out: bfloat16 [384, 384], P('col'), may hold values from -0.3125 to 0.3125
Outputs:
- pair_out: bfloat16 [256, 2048, 128], P('row', 'col')
- single_out: bfloat16 [256, 384], P('row')
The draws below stay inside these ranges and needn't reach their ends.
Inputs may be any that keep to these rules, and one draw needn't show every extreme that they name: `token_mask`: each entry is 0 or 1; the first token of every aligned block of 64 tokens is 1.
All inputs are finite; a program needn't handle non-finite values.
Results may differ from the reference program's by a relative error of at most 0.0075.
Values may be sent and summed in bfloat16 or wider, within the bound.
A program may use at most 64 MiB of HBM per device.

```python
import math
import jax
import jax.numpy as jnp
import numpy as np
from jax import lax

D_PAIR = 128
D_SINGLE = 384
HEADS = 16
TRANS_HIDDEN = 512
TOK_DEV = 64
SLAB_DEV = 8
HEAD_DIM = 24
TOKENS = 2048
SLAB = 256
N_ROW = 32


def draw_token_mask(key, part):
    key = jax.random.fold_in(key, 11)
    coins = jax.random.randint(key, (TOKENS,), 0, 4)
    places = jnp.arange(TOKENS)
    return jnp.where(places % TOK_DEV == 0, 1, (coins < 3).astype(jnp.int32)).astype(jnp.int32)


def shard_levels(own_key, extent, pieces, low, top_value):
    loudness, own = 1.0, jax.random.fold_in(own_key, 6)
    for dim, parts in pieces:
        heights = jnp.exp(jax.random.uniform(jax.random.fold_in(own, dim), (parts,), jnp.float32, low / len(pieces), top_value / len(pieces)))
        loudness = loudness * jnp.repeat(heights, extent[dim] // parts).reshape([-1 if axis == dim else 1 for axis in range(len(extent))])
    return loudness


def split_up(number_of, total, bound, lean):
    weights = [(1 << 20) // math.isqrt(rank ** lean) + 1 for rank in range(2, number_of + 1)]
    surplus, holding = total - bound - (number_of - 1), [1] * (number_of - 1)
    while surplus > 0:
        candidates = [i for i in range(number_of - 1) if holding[i] < bound]
        pool, budget = sum([weights[i] for i in candidates]), surplus
        for i in candidates:
            more = min(bound - holding[i], max(1, budget * weights[i] // pool), surplus)
            holding[i] = holding[i] + more
            surplus = surplus - more
    return np.array([bound] + holding)


def uneven_parts(key, amount, total, most, skew):
    if amount == 2:
        one = jax.random.randint(key, (), max(1, total - most), min(most, total - 1) + 1)
        return jnp.stack([one, total - one])
    tallies = jnp.asarray(split_up(amount, total, most, skew), jnp.int32)
    pairs = (amount - 1) // 2
    source_of, receiver = tallies[1:1 + 2 * pairs:2], tallies[2:2 + 2 * pairs:2]
    margin = jnp.minimum(source_of - 1, most - receiver)
    moved = jax.random.randint(jax.random.fold_in(key, 1), (pairs,), 0, 1 << 20) % (margin + 1)
    tallies = tallies.at[1:1 + 2 * pairs:2].set(source_of - moved).at[2:2 + 2 * pairs:2].set(receiver + moved)
    return tallies[jax.random.permutation(jax.random.fold_in(key, 2), amount)]


def normal_values(rng, extent, deviation, limit, shards=(), held_as=jnp.bfloat16):
    level = shard_levels(rng, extent, shards, -0.22, 0.18) if shards else 1.0
    array = jax.random.normal(rng, extent, jnp.float32) * deviation * level
    return jnp.minimum(jnp.maximum(array, -limit), limit).astype(held_as)


def setup_inputs(seed: int = 0) -> dict:
    streams_of = jax.random.split(jax.random.key(seed), 15)
    return {
        "pair": normal_values(streams_of[0], (SLAB, TOKENS, D_PAIR), 1.0, 6.0, ((0, 32), (1, 16))),
        "panel_left": normal_values(streams_of[1], (SLAB, TOKENS, D_PAIR), 1.0, 6.0, ((0, 32), (1, 16))),
        "panel_right": normal_values(streams_of[2], (TOKENS, TOKENS, D_PAIR), 1.0, 6.0, ((0, 32), (1, 16))),
        "single": normal_values(streams_of[3], (TOKENS, D_SINGLE), 1.0, 6.0, ((0, 32),)),
        "token_mask": draw_token_mask(jax.random.fold_in(streams_of[14], 71), 0),
        "chain_ids": jnp.searchsorted(jnp.cumsum(uneven_parts(streams_of[5], 4, TOKENS, TOKENS // 2, 0)), jnp.arange(TOKENS), side="right").astype(jnp.int32),
        "w_tri_gate": normal_values(streams_of[6], (D_PAIR, D_PAIR), D_PAIR ** -0.5, 0.5),
        "w_tri_out": normal_values(streams_of[7], (D_PAIR, D_PAIR), D_PAIR ** -0.5, 0.5),
        "w_trans_in": normal_values(streams_of[8], (D_PAIR, 2 * TRANS_HIDDEN), D_PAIR ** -0.5, 0.5),
        "w_trans_down": normal_values(streams_of[9], (TRANS_HIDDEN, D_PAIR), TRANS_HIDDEN ** -0.5, 0.25),
        "w_bias": normal_values(streams_of[10], (D_PAIR, HEADS), 0.25, 1.5),
        "chain_bias": jnp.clip(jax.random.uniform(streams_of[11], (HEADS,), jnp.float32, -2.0, 2.0), -2.0, 2.0),
        "w_attn": normal_values(streams_of[12], (4, D_SINGLE, D_SINGLE), D_SINGLE ** -0.5, 0.3125, ((2, 16),)),
        "w_attn_out": normal_values(streams_of[13], (D_SINGLE, D_SINGLE), D_SINGLE ** -0.5, 0.3125, ((0, 16),)),
    }


epsilon = 1e-05

def layer_norm(values, axis):
    mean_val = lax.optimization_barrier(jnp.mean(values, axis=axis, keepdims=True))
    centred = values - mean_val
    variance = lax.optimization_barrier(jnp.mean(centred * centred, axis=axis, keepdims=True))
    return centred * lax.rsqrt(variance + epsilon)

def reference(pair, panel_left, panel_right, single, token_mask, chain_ids, w_tri_gate, w_tri_out, w_trans_in, w_trans_down, w_bias, chain_bias, w_attn, w_attn_out):
    left_first = jnp.transpose(panel_left, (2, 0, 1))
    right_first = jnp.transpose(panel_right, (2, 0, 1))

    def one_channel(operands):
        left_mat, right_mat = operands
        return jnp.dot(left_mat, right_mat.T, preferred_element_type=jnp.float32).astype(jnp.bfloat16)
    triangle = jnp.transpose(lax.map(one_channel, (left_first, right_first)), (1, 2, 0))
    places = jnp.arange(SLAB)
    slab_tokens = places // SLAB_DEV * TOK_DEV + places % SLAB_DEV
    slab_chain = chain_ids[slab_tokens]
    hidden_width = w_trans_down.shape[0]

    def pair_rows(operands):
        pair_block, tri_block, chain_block = operands
        pair_norm = layer_norm(pair_block.astype(jnp.float32), -1).astype(jnp.bfloat16)
        gate_tri = jax.nn.sigmoid(jnp.dot(pair_norm, w_tri_gate, preferred_element_type=jnp.float32))
        tri_norm = layer_norm(tri_block.astype(jnp.float32), -1).astype(jnp.bfloat16)
        pair_mid = pair_block.astype(jnp.float32) + gate_tri * jnp.dot(tri_norm, w_tri_out, preferred_element_type=jnp.float32)
        trans_in = layer_norm(pair_mid, -1).astype(jnp.bfloat16)
        both_parts = jnp.dot(trans_in, w_trans_in, preferred_element_type=jnp.float32)
        trans_act = (jax.nn.silu(both_parts[..., :hidden_width]) * both_parts[..., hidden_width:]).astype(jnp.bfloat16)
        pair_new = (pair_mid + jnp.dot(trans_act, w_trans_down, preferred_element_type=jnp.float32)).astype(jnp.bfloat16)
        bias_norm = layer_norm(pair_new.astype(jnp.float32), -1).astype(jnp.bfloat16)
        linear_part = jnp.transpose(jnp.dot(bias_norm, w_bias, preferred_element_type=jnp.float32), (2, 0, 1))
        same_chain = (chain_block[:, None] == chain_ids[None, :]).astype(jnp.float32)
        return (pair_new, linear_part + chain_bias[:, None, None] * same_chain[None])
    pair_blocks = pair.reshape(N_ROW, SLAB_DEV, TOKENS, D_PAIR)
    tri_blocks = triangle.reshape(N_ROW, SLAB_DEV, TOKENS, D_PAIR)
    chain_blocks = slab_chain.reshape(N_ROW, SLAB_DEV)
    pair_new, bias_blocks = lax.map(pair_rows, (pair_blocks, tri_blocks, chain_blocks))
    pair_out = pair_new.reshape(SLAB, TOKENS, D_PAIR)
    pair_bias = jnp.transpose(bias_blocks, (1, 0, 2, 3)).reshape(HEADS, SLAB, TOKENS)
    single_norm = layer_norm(single.astype(jnp.float32), -1).astype(jnp.bfloat16)
    query_in = single_norm[slab_tokens]
    score_scale = HEAD_DIM ** (-0.5)
    queries = (jnp.dot(query_in, w_attn[0], preferred_element_type=jnp.float32) * score_scale).astype(jnp.bfloat16)
    keys_all = jnp.dot(single_norm, w_attn[1], preferred_element_type=jnp.float32).astype(jnp.bfloat16)
    values_all = jnp.dot(single_norm, w_attn[2], preferred_element_type=jnp.float32).astype(jnp.bfloat16)
    gate_single = jax.nn.sigmoid(jnp.dot(query_in, w_attn[3], preferred_element_type=jnp.float32))
    key_mask = token_mask.astype(jnp.float32)
    heads_queries = jnp.transpose(queries.reshape(SLAB, HEADS, HEAD_DIM), (1, 0, 2))
    heads_keys = jnp.transpose(keys_all.reshape(TOKENS, HEADS, HEAD_DIM), (1, 0, 2))
    heads_values = jnp.transpose(values_all.reshape(TOKENS, HEADS, HEAD_DIM), (1, 0, 2))

    def one_head(operands):
        head_query, head_key, head_value, head_bias = operands
        scores = jnp.dot(head_query, head_key.T, preferred_element_type=jnp.float32) + head_bias
        weights = jnp.exp(scores) * key_mask[None, :]
        denominator = lax.optimization_barrier(jnp.sum(weights, axis=1))
        numerator = jnp.dot(weights.astype(jnp.bfloat16), head_value, preferred_element_type=jnp.float32)
        return numerator / denominator[:, None]
    attended = lax.map(one_head, (heads_queries, heads_keys, heads_values, pair_bias))
    attended = jnp.transpose(attended, (1, 0, 2)).reshape(SLAB, D_SINGLE)
    gated = (gate_single * attended).astype(jnp.bfloat16)
    single_out = (single[slab_tokens].astype(jnp.float32) + jnp.dot(gated, w_attn_out, preferred_element_type=jnp.float32)).astype(jnp.bfloat16)
    return (pair_out, single_out)
```

```python
import jax
import jax.numpy as jnp
from jax import lax
from jax.experimental import pallas as pl
from jax.experimental.pallas import tpu as pltpu
from jax.sharding import PartitionSpec as P

HEAD_DIM = 24
HEADS = 16
NZ = 8
NY = 4
NQ = 16
GROUP = NY * NQ
MESH = pl.DeviceIdType.MESH

epsilon = 1e-05


def layer_norm(values, axis):
    mean_val = jnp.mean(values, axis=axis, keepdims=True)
    centred = values - mean_val
    variance = jnp.mean(centred * centred, axis=axis, keepdims=True)
    return centred * lax.rsqrt(variance + epsilon)


def remote(src, dst, send, recv, row, col):
    return pltpu.make_async_remote_copy(
        src_ref=src, dst_ref=dst, send_sem=send, recv_sem=recv, device_id=(row, col), device_id_type=MESH
    )


def exchange_kernel(
    lt, rt, kv, qg, wo, t_out, kv_all, qg_all, wo_all, lbuf, rbuf, tsend,
    own_sem, l_send, l_recv, r_send, r_recv, z_send, z_recv, k_send, k_recv, q_send, q_recv, w_send, w_recv, t_send, t_recv,
):
    row = lax.axis_index("row")
    col = lax.axis_index("col")
    z = row // NY
    yh = row % NY
    me = yh * NQ + col

    def group_device(m):
        return z * NY + m // NQ, m % NQ

    def others(body):
        def step(n, carry):
            body((me + n) % GROUP)
            return carry

        lax.fori_loop(1, GROUP, step, 0)

    def l_block(m):
        source_row, source_col = group_device(m)
        return lbuf.at[pl.ds(source_row * 16, 16), pl.ds(source_col * 128, 128)]

    def r_block(m):
        return rbuf.at[:, pl.ds((m // NQ) * 64, 64), pl.ds((m % NQ) * 128, 128)]

    def l_copy(m, slot):
        return remote(lt.at[m], l_block(slot), l_send.at[m], l_recv.at[slot], *group_device(m))

    def r_copy(m, slot):
        return remote(rt.at[pl.ds(m * 2, 2)], r_block(slot), r_send.at[m], r_recv.at[slot], *group_device(m))

    l_own = pltpu.make_async_copy(lt.at[me], l_block(me), own_sem.at[0])
    l_own.start()
    others(lambda m: l_copy(m, me).start())

    home = row // 2
    k_slot = (row % 2) * NQ + col
    k_own = pltpu.make_async_copy(kv, kv_all.at[k_slot], own_sem.at[1])

    def k_copy(target, slot):
        return remote(kv, kv_all.at[slot], k_send.at[target], k_recv.at[slot], target, home)

    def k_start(n, carry):
        target = (row + n) % (NZ * NY)
        stays = (n == 0) & (home == col)

        @pl.when(stays)
        def _():
            k_own.start()

        @pl.when(jnp.logical_not(stays))
        def _():
            k_copy(target, k_slot).start()

        return carry

    lax.fori_loop(0, NZ * NY, k_start, 0)

    q_own = pltpu.make_async_copy(qg, qg_all.at[col], own_sem.at[2])
    w_own = pltpu.make_async_copy(wo, wo_all.at[col], own_sem.at[3])
    q_own.start()
    w_own.start()

    def q_copy(target, slot):
        return remote(qg, qg_all.at[slot], q_send.at[target], q_recv.at[slot], row, target)

    def w_copy(target, slot):
        return remote(wo, wo_all.at[slot], w_send.at[target], w_recv.at[slot], row, target)

    def q_start(n, carry):
        target = (col + n) % NQ
        q_copy(target, col).start()
        w_copy(target, col).start()
        return carry

    lax.fori_loop(1, NQ, q_start, 0)

    r_own = pltpu.make_async_copy(rt.at[pl.ds(me * 2, 2)], r_block(me), own_sem.at[4])
    r_own.start()
    others(lambda m: r_copy(m, me).start())

    l_own.wait()
    others(lambda m: l_copy(m, m).wait_recv())

    def z_block(plane):
        return lbuf.at[pl.ds(plane * 64, 64), :]

    def z_copy(plane, way, target_z):
        return remote(z_block(plane), z_block(plane), z_send.at[way, plane], z_recv.at[plane], target_z * NY + yh, col)

    up = (z + 1) % NZ
    down = (z + NZ - 1) % NZ
    for step in range(4):
        if step:
            z_copy((z + NZ - step) % NZ, 0, up).wait_recv()
        z_copy((z + NZ - step) % NZ, 0, up).start()
        if step < 3:
            if step:
                z_copy((z + step) % NZ, 1, down).wait_recv()
            z_copy((z + step) % NZ, 1, down).start()
    z_copy((z + 4) % NZ, 0, up).wait_recv()
    z_copy((z + 3) % NZ, 1, down).wait_recv()

    r_own.wait()
    others(lambda m: r_copy(m, m).wait_recv())

    def multiply(tile, carry):
        start = pl.multiple_of(tile * 128, 128)
        rows = lbuf[pl.ds(start, 128), :]
        dims = (((1,), (1,)), ((), ()))
        first = lax.dot_general(rows, rbuf[0], dims, preferred_element_type=jnp.float32)
        second = lax.dot_general(rows, rbuf[1], dims, preferred_element_type=jnp.float32)
        channel = (lax.broadcasted_iota(jnp.int32, first.shape, 0) // 8) % 2
        both = jnp.where(channel == 0, first, second).astype(jnp.bfloat16)
        for half in range(2):
            tsend[half, pl.ds(tile * 8, 8)] = both[:, half * 128 : half * 128 + 128].reshape(8, 16, 128)
        return carry

    lax.fori_loop(0, 4, multiply, 0)

    t_own = pltpu.make_async_copy(tsend.at[col % 2, row], t_out.at[me], own_sem.at[5])

    def t_copy(m, slot):
        return remote(tsend.at[m % 2, m // 2], t_out.at[slot], t_send.at[m], t_recv.at[slot], m // 2, 2 * z + m % 2)

    def t_stays(m):
        return (m // 2 == row) & (2 * z + m % 2 == col)

    def t_start(n, carry):
        m = (me + n) % GROUP
        stays = t_stays(m)

        @pl.when(stays)
        def _():
            t_own.start()

        @pl.when(jnp.logical_not(stays))
        def _():
            t_copy(m, me).start()

        return carry

    lax.fori_loop(0, GROUP, t_start, 0)

    others(lambda m: l_copy(m, me).wait_send())
    others(lambda m: r_copy(m, me).wait_send())
    for step in range(4):
        z_copy((z + NZ - step) % NZ, 0, up).wait_send()
        if step < 3:
            z_copy((z + step) % NZ, 1, down).wait_send()

    def k_wait(n, carry):
        target = (row + n) % (NZ * NY)
        stays = (n == 0) & (home == col)

        @pl.when(jnp.logical_not(stays))
        def _():
            k_copy(target, k_slot).wait_send()

        from_self = (2 * col + n // NQ == row) & (n % NQ == col)

        @pl.when(from_self)
        def _():
            k_own.wait()

        @pl.when(jnp.logical_not(from_self))
        def _():
            k_copy(n, n).wait_recv()

        return carry

    lax.fori_loop(0, NZ * NY, k_wait, 0)
    q_own.wait()
    w_own.wait()

    def q_wait(n, carry):
        target = (col + n) % NQ
        q_copy(target, col).wait_send()
        w_copy(target, col).wait_send()
        q_copy(target, target).wait_recv()
        w_copy(target, target).wait_recv()
        return carry

    lax.fori_loop(1, NQ, q_wait, 0)

    def t_wait(s, carry):
        from_self = (col // 2 == z) & (s == me)

        @pl.when(from_self)
        def _():
            t_own.wait()

        @pl.when(jnp.logical_not(from_self))
        def _():
            t_copy(s, s).wait_recv()

        @pl.when(jnp.logical_not(t_stays(s)))
        def _():
            t_copy(s, me).wait_send()

        return carry

    lax.fori_loop(0, GROUP, t_wait, 0)


def exchange(lt, rt, kv, qg, wo):
    dma = pltpu.SemaphoreType.DMA
    return pl.pallas_call(
        exchange_kernel,
        out_shape=(
            jax.ShapeDtypeStruct((GROUP, 16, 128), jnp.bfloat16),
            jax.ShapeDtypeStruct((2 * NQ, 32, 128), jnp.bfloat16),
            jax.ShapeDtypeStruct((NQ, 8, 128), jnp.float32),
            jax.ShapeDtypeStruct((NQ, 24, 384), jnp.float32),
        ),
        in_specs=[pl.BlockSpec(memory_space=pl.ANY)] * 5,
        out_specs=(pl.BlockSpec(memory_space=pl.ANY),) * 4,
        scratch_shapes=[
            pltpu.VMEM((512, 2048), jnp.bfloat16),
            pltpu.VMEM((2, 256, 2048), jnp.bfloat16),
            pltpu.VMEM((2, 32, 16, 128), jnp.bfloat16),
            dma((6,)),
            dma((GROUP,)),
            dma((GROUP,)),
            dma((GROUP,)),
            dma((GROUP,)),
            dma((2, NZ)),
            dma((NZ,)),
            dma((2 * NQ,)),
            dma((2 * NQ,)),
            dma((NQ,)),
            dma((NQ,)),
            dma((NQ,)),
            dma((NQ,)),
            dma((GROUP,)),
            dma((GROUP,)),
        ],
        compiler_params=pltpu.CompilerParams(has_side_effects=True, vmem_limit_bytes=32 * 1024 * 1024),
        name="exchange",
    )(lt, rt, kv, qg, wo)


def finish_kernel(part, gate, wo, single, out, slots, own_sem, send, recv):
    row = lax.axis_index("row")
    col = lax.axis_index("col")

    def copy(target, slot):
        return remote(part, slots.at[slot], send.at[target], recv.at[slot], row, target)

    own = pltpu.make_async_copy(part, slots.at[col], own_sem)
    own.start()

    def start(n, carry):
        copy((col + n) % NQ, col).start()
        return carry

    lax.fori_loop(1, NQ, start, 0)
    own.wait()

    def wait(n, carry):
        target = (col + n) % NQ
        copy(target, target).wait_recv()
        copy(target, col).wait_send()
        return carry

    lax.fori_loop(1, NQ, wait, 0)
    total = slots[0]
    for n in range(1, NQ):
        total = total + slots[n]
    attended = total[:8] / total[8:]
    gated = (gate[...] * attended).astype(jnp.bfloat16)
    mixed = jnp.dot(gated, wo[...].astype(jnp.bfloat16), preferred_element_type=jnp.float32)
    out[...] = (single[...].astype(jnp.float32) + mixed).astype(jnp.bfloat16)


def finish(part, gate, wo, single):
    dma = pltpu.SemaphoreType.DMA
    return pl.pallas_call(
        finish_kernel,
        out_shape=jax.ShapeDtypeStruct((8, 384), jnp.bfloat16),
        in_specs=[pl.BlockSpec(memory_space=pltpu.VMEM)] * 4,
        out_specs=pl.BlockSpec(memory_space=pltpu.VMEM),
        scratch_shapes=[pltpu.VMEM((NQ, 16, 384), jnp.float32), dma, dma((NQ,)), dma((NQ,))],
        compiler_params=pltpu.CompilerParams(has_side_effects=True, vmem_limit_bytes=16 * 1024 * 1024),
        name="finish",
    )(part, gate, wo, single)


def local(
    pair,
    panel_left,
    panel_right,
    single,
    token_mask,
    chain_ids,
    w_tri_gate,
    w_tri_out,
    w_trans_in,
    w_trans_down,
    w_bias,
    chain_bias,
    w_attn,
    w_attn_out,
):
    rows_own = pair.shape[0]
    cols_own = pair.shape[1]
    lt = jnp.transpose(panel_left, (2, 0, 1)).reshape(GROUP, 16, 128)
    rt = jnp.transpose(panel_right, (2, 0, 1))

    single_norm = layer_norm(single.astype(jnp.float32), -1).astype(jnp.bfloat16)
    query_in = single_norm[:rows_own]
    score_scale = HEAD_DIM ** (-0.5)
    kv_own = jnp.dot(
        single_norm, jnp.concatenate((w_attn[1], w_attn[2]), axis=1), preferred_element_type=jnp.float32
    ).astype(jnp.bfloat16)
    marks = jnp.stack((token_mask, chain_ids), axis=1).astype(jnp.bfloat16)
    kv = jnp.concatenate(
        (kv_own[:32], kv_own[32:], marks[:32], marks[32:], jnp.zeros((32, 28), jnp.bfloat16)), axis=1
    )
    query_own = (jnp.dot(query_in, w_attn[0], preferred_element_type=jnp.float32) * score_scale).astype(jnp.bfloat16)
    gate_own = jax.nn.sigmoid(jnp.dot(query_in, w_attn[3], preferred_element_type=jnp.float32))
    qg = jnp.concatenate((query_own.astype(jnp.float32), gate_own, jnp.zeros((8, 80), jnp.float32)), axis=1)

    t_out, kv_all, qg_all, wo_all = exchange(lt, rt, kv, qg, w_attn_out.astype(jnp.float32))

    tri_full = t_out.reshape(128, rows_own, cols_own)
    pair_norm = layer_norm(pair.astype(jnp.float32), -1).astype(jnp.bfloat16)
    gate_tri = jax.nn.sigmoid(jnp.dot(pair_norm, w_tri_gate, preferred_element_type=jnp.float32))
    tri_norm = layer_norm(tri_full.astype(jnp.float32), 0).astype(jnp.bfloat16)
    projected = jnp.einsum("cij,cd->ijd", tri_norm, w_tri_out, preferred_element_type=jnp.float32)
    pair_mid = pair.astype(jnp.float32) + gate_tri * projected
    hidden_width = w_trans_down.shape[0]
    trans_in = layer_norm(pair_mid, -1).astype(jnp.bfloat16)
    both_parts = jnp.dot(trans_in, w_trans_in, preferred_element_type=jnp.float32)
    trans_act = (
        jax.nn.silu(both_parts[..., :hidden_width]) * both_parts[..., hidden_width:]
    ).astype(jnp.bfloat16)
    pair_out = (
        pair_mid + jnp.dot(trans_act, w_trans_down, preferred_element_type=jnp.float32)
    ).astype(jnp.bfloat16)
    bias_norm = layer_norm(pair_out.astype(jnp.float32), -1).astype(jnp.bfloat16)

    by_head = kv_all.reshape(2, HEADS, 32, 128)
    halves = jnp.stack((by_head[..., :48], by_head[..., 48:96]), axis=2)
    tokens = jnp.transpose(halves, (1, 0, 2, 3, 4)).reshape(HEADS, cols_own, 48)
    keys_heads = tokens[..., :HEAD_DIM]
    values_heads = tokens[..., HEAD_DIM:]
    marks_all = by_head[:, 0, :, 96:100].astype(jnp.float32)
    mask_cols = jnp.stack((marks_all[..., 0], marks_all[..., 2]), axis=1).reshape(cols_own)
    chain_cols = jnp.stack((marks_all[..., 1], marks_all[..., 3]), axis=1).reshape(cols_own)
    chain_rows = chain_ids[:rows_own].astype(jnp.float32)

    linear_part = jnp.einsum("ijc,ch->hij", bias_norm, w_bias, preferred_element_type=jnp.float32)
    same_chain = (chain_rows[:, None] == chain_cols[None, :]).astype(jnp.float32)
    bias_tile = linear_part + chain_bias[:, None, None] * same_chain[None]
    queries = qg_all[..., :HEAD_DIM].astype(jnp.bfloat16)
    gate = jnp.transpose(qg_all[..., HEAD_DIM : 2 * HEAD_DIM], (1, 0, 2)).reshape(rows_own, HEADS * HEAD_DIM)
    scores = (
        jnp.einsum("hid,hjd->hij", queries, keys_heads, preferred_element_type=jnp.float32) + bias_tile
    )
    weights = jnp.exp(scores) * mask_cols[None, None, :]
    denominator = jnp.sum(weights, axis=2)
    numerator = jnp.einsum(
        "hij,hjd->ihd", weights.astype(jnp.bfloat16), values_heads, preferred_element_type=jnp.float32
    ).reshape(rows_own, HEADS * HEAD_DIM)
    denominator = jnp.repeat(jnp.transpose(denominator), HEAD_DIM, axis=1)
    part = jnp.concatenate((numerator, denominator), axis=0)
    single_out = finish(part, gate, wo_all.reshape(HEADS * HEAD_DIM, 384), single[:rows_own])
    return (pair_out, single_out)


def solution(mesh):
    in_specs = (
        P("row", "col", None),
        P("row", "col", None),
        P("row", "col", None),
        P("row", None),
        P("row"),
        P("row"),
        P(),
        P(),
        P(),
        P(),
        P(),
        P(),
        P(None, None, "col"),
        P("col", None),
    )
    out_specs = (P("row", "col", None), P("row", None))
    return jax.shard_map(local, mesh=mesh, in_specs=in_specs, out_specs=out_specs, check_vma=False)
```

```python
import jax
import jax.numpy as jnp
from jax import lax
from jax.experimental import pallas as pl
from jax.experimental.pallas import tpu as pltpu
from jax.sharding import PartitionSpec as P

HEAD_DIM = 24
HEADS = 16
NZ = 8
NY = 4
NQ = 16
GROUP = NY * NQ
SLOT = 32
WIDE = HEADS * SLOT
MESH = pl.DeviceIdType.MESH
EARLY = 24

epsilon = 1e-05


def layer_norm(values, axis):
    mean_val = jnp.mean(values, axis=axis, keepdims=True)
    centred = values - mean_val
    variance = jnp.mean(centred * centred, axis=axis, keepdims=True)
    return centred * lax.rsqrt(variance + epsilon)


def remote(src, dst, send, recv, row, col):
    return pltpu.make_async_remote_copy(
        src_ref=src, dst_ref=dst, send_sem=send, recv_sem=recv, device_id=(row, col), device_id_type=MESH
    )


def dot(a, b, over_a, over_b):
    return lax.dot_general(a, b, (((over_a,), (over_b,)), ((), ())), preferred_element_type=jnp.float32)


def block_kernel(
    lt, rt, pair, single, w_gate, w_out, w_in, w_down, mask_any, chain_any, bias_any, w_bias_any, w_attn_any, w_attn_out_any,
    pair_out, single_out,
    lbuf, rbuf, tsend, tin, tin32, gate_tri, kv_msg, kv_all, qg_msg, qg_all, wo_msg, wo_all, proj_in, square,
    q_full, gate_full, bias_all, part, parts, mask_in, chain_in, chain_bias, bias_weights, w_attn, w_attn_out,
    values_low, own_values_kept, own_sum_kept, mask_kept,
    own_sem, in_sem, l_send, l_recv, r_send, r_recv, z_send, z_recv, k_send, k_recv, kz_send, kz_recv,
    q_send, q_recv, w_send, w_recv, t_send, t_recv, p_send, p_recv,
):
    row = lax.axis_index("row")
    col = lax.axis_index("col")
    z = row // NY
    yh = row % NY
    me = yh * NQ + col
    up = lax.rem(z + 1, NZ)
    down = lax.rem(z + NZ - 1, NZ)

    def group_device(m):
        return z * NY + lax.div(m, NQ), lax.rem(m, NQ)

    def others(body, start=1, stop=GROUP):
        def step(n, carry):
            body(lax.rem(me + n, GROUP))
            return carry

        lax.fori_loop(start, stop, step, 0)

    barrier = pltpu.get_barrier_semaphore()

    def greet(m):
        pl.semaphore_signal(barrier, inc=1, device_id=group_device(m), device_id_type=MESH)

    for plane in (up, down):
        pl.semaphore_signal(barrier, inc=1, device_id=(plane * NY + yh, col), device_id_type=MESH)
    others(greet)

    home = lax.div(row, 2)
    k_slot = lax.rem(row, 2) * NQ + col
    k_plane = lax.div(k_slot, 4)

    def k_source(n):
        return 2 * col + lax.div(z, 4), 4 * lax.rem(z, 4) + n

    def k_from_self(n):
        source_row, source_col = k_source(n)
        return (source_row == row) & (source_col == col)

    def k_to_self(n):
        return (k_plane == z) & (n == yh) & (home == col)

    def k_greet(n, carry):
        @pl.when(jnp.logical_not(k_from_self(n)))
        def _():
            pl.semaphore_signal(barrier, inc=1, device_id=k_source(n), device_id_type=MESH)

        return carry

    lax.fori_loop(0, 4, k_greet, 0)

    inputs = [
        pltpu.make_async_copy(source, target, in_sem.at[n])
        for n, (source, target) in enumerate(
            (
                (w_attn_any, w_attn), (mask_any, mask_in), (chain_any, chain_in), (bias_any, chain_bias),
                (w_bias_any, bias_weights), (w_attn_out_any, w_attn_out),
            )
        )
    ]
    for copy in inputs:
        copy.start()

    def l_block(m):
        source_row, source_col = group_device(m)
        return lbuf.at[pl.ds(source_row * 16, 16), pl.ds(source_col * 128, 128)]

    def r_block(m):
        return rbuf.at[m]

    def l_copy(m, slot):
        return remote(lt.at[m], l_block(slot), l_send.at[m], l_recv.at[slot], *group_device(m))

    def r_copy(m, slot):
        return remote(rt.at[pl.ds(m * 2, 2)], r_block(slot), r_send.at[m], r_recv.at[slot], *group_device(m))

    l_own = pltpu.make_async_copy(lt.at[me], l_block(me), own_sem.at[0])
    r_own = pltpu.make_async_copy(rt.at[pl.ds(me * 2, 2)], r_block(me), own_sem.at[4])
    l_own.start()
    r_own.start()

    proj_in[...] = jnp.zeros_like(proj_in)
    wo_msg[...] = jnp.zeros_like(wo_msg)
    qg_msg[...] = jnp.zeros_like(qg_msg)
    single_norm = layer_norm(single[...].astype(jnp.float32), -1).astype(jnp.bfloat16)

    remaining = k_to_self(yh)
    pl.semaphore_wait(barrier, GROUP + 5 - remaining.astype(jnp.int32))
    others(lambda m: r_copy(m, me).start(), 1, 9)
    others(lambda m: l_copy(m, me).start())
    others(lambda m: r_copy(m, me).start(), 9, EARLY)

    for copy in inputs:
        copy.wait()
    for place, which in enumerate((1, 2, 0, 3)):
        proj_in[place * SLOT : place * SLOT + HEAD_DIM, :] = w_attn[which].astype(jnp.float32)
    proj = proj_in[...].astype(jnp.bfloat16)
    key_value = dot(proj[0 : 2 * SLOT], single_norm, 1, 1)
    square[0:SLOT, 0:64] = key_value[0:SLOT]
    square[0:SLOT, 64:128] = key_value[SLOT : 2 * SLOT]
    square[HEAD_DIM : HEAD_DIM + 1, 0:64] = mask_in[...].astype(jnp.float32)
    square[HEAD_DIM : HEAD_DIM + 1, 64:128] = chain_in[...].astype(jnp.float32)
    kv_msg[...] = square[0:SLOT, :].astype(jnp.bfloat16)
    first_rows = dot(single_norm[0:16], proj[2 * SLOT : 4 * SLOT], 1, 1)[0:8]
    scaled = (first_rows * (HEAD_DIM ** (-0.5))).astype(jnp.bfloat16).astype(jnp.float32)
    lane = lax.broadcasted_iota(jnp.int32, (8, 2 * SLOT), 1)
    qg_msg[:, 0 : 2 * SLOT] = jnp.where(lane < SLOT, scaled, jax.nn.sigmoid(first_rows))

    k_own = pltpu.make_async_copy(kv_msg, kv_all.at[k_slot], own_sem.at[1])

    def k_copy(n, slot):
        return remote(kv_msg, kv_all.at[slot], k_send.at[n], k_recv.at[lax.rem(slot, 4)], k_plane * NY + n, home)

    def k_start(n, carry):
        stays = k_to_self(n)

        @pl.when(stays)
        def _():
            k_own.start()

        @pl.when(jnp.logical_not(stays))
        def _():
            k_copy(n, k_slot).start()

        return carry

    lax.fori_loop(0, 4, k_start, 0)

    def q_copy(target, slot):
        return remote(qg_msg, qg_all.at[slot], q_send.at[target], q_recv.at[slot], row, target)

    q_own = pltpu.make_async_copy(qg_msg, qg_all.at[col], own_sem.at[2])
    q_own.start()

    def q_start(n, carry):
        target = lax.rem(col + n, NQ)
        q_copy(target, col).start()
        return carry

    lax.fori_loop(1, NQ, q_start, 0)
    others(lambda m: r_copy(m, me).start(), EARLY, GROUP)

    l_own.wait()
    others(lambda m: l_copy(m, m).wait_recv())

    def z_copy(plane, way, target_z):
        block = lbuf.at[pl.ds(plane * 64, 64), :]
        return remote(block, block, z_send.at[way, plane], z_recv.at[plane], target_z * NY + yh, col)

    def kz_copy(plane, way, target_z):
        block = kv_all.at[pl.ds(plane * 4, 4)]
        return remote(block, block, kz_send.at[way, plane], kz_recv.at[plane], target_z * NY + yh, col)

    def plane_at(offset):
        return lax.rem(z + NZ + offset, NZ)

    def k_wait(n, carry):
        from_self = k_from_self(n)

        @pl.when(from_self)
        def _():
            k_own.wait()

        @pl.when(jnp.logical_not(from_self))
        def _():
            k_copy(0, z * 4 + n).wait_recv()

        return carry

    lax.fori_loop(0, 4, k_wait, 0)

    def ring_step(step):
        for copy in (z_copy, kz_copy):
            if step:
                copy(plane_at(-step), 0, up).wait_recv()
            copy(plane_at(-step), 0, up).start()
            if step < 3:
                if step:
                    copy(plane_at(step), 1, down).wait_recv()
                copy(plane_at(step), 1, down).start()

    ring_step(0)

    proj_in[0:SLOT, :] = jnp.zeros((SLOT, 384), jnp.float32)
    proj_in[0:HEAD_DIM, :] = w_attn_out[...].astype(jnp.float32)
    wo_msg[...] = proj_in[0:SLOT, :].astype(jnp.bfloat16)
    square[...] = jnp.zeros_like(square)
    square[:, 0:HEADS] = jnp.broadcast_to(chain_bias[...], (128, HEADS))
    chain_heads = square[...].T[0:HEADS]

    ring_step(1)

    def gates(tile, carry):
        rows = pl.ds(pl.multiple_of(tile * 256, 256), 256)
        pair_norm = layer_norm(pair[rows, :].astype(jnp.float32), -1).astype(jnp.bfloat16)
        gate_tri[rows, :] = jax.nn.sigmoid(dot(pair_norm, w_gate[...], 1, 0))
        return carry

    lax.fori_loop(0, 4, gates, 0)

    ring_step(2)
    ring_step(3)
    for copy in (z_copy, kz_copy):
        copy(plane_at(4), 0, up).wait_recv()
        copy(plane_at(3), 1, down).wait_recv()
    q_own.wait()

    def q_wait(n, carry):
        target = lax.rem(col + n, NQ)
        q_copy(target, col).wait_send()
        q_copy(target, target).wait_recv()
        return carry

    lax.fori_loop(1, NQ, q_wait, 0)
    for head in range(HEADS):
        lanes = slice(head * SLOT, head * SLOT + SLOT)
        q_full[:, lanes] = qg_all[head, :, 0:SLOT]
        gate_full[:, lanes] = qg_all[head, :, SLOT : 2 * SLOT]


    low = kv_all[0:HEADS].astype(jnp.float32).reshape(WIDE, 128)
    high = kv_all[HEADS : 2 * HEADS].astype(jnp.float32).reshape(WIDE, 128)
    lane = lax.broadcasted_iota(jnp.int32, (WIDE, 128), 1)
    keys = jnp.where(lane < 64, low, pltpu.roll(high, 64, 1))
    values = jnp.where(lane < 64, pltpu.roll(low, 64, 1), high)
    mask_cols = keys[HEAD_DIM : HEAD_DIM + 1, :]
    chain_cols = values[HEAD_DIM : HEAD_DIM + 1, :]
    head_of_row = lax.broadcasted_iota(jnp.int32, (HEADS, WIDE), 0)
    lane_wide = lax.broadcasted_iota(jnp.int32, (HEADS, WIDE), 1)
    own_block = head_of_row == lax.div(lane_wide, SLOT)
    depth = lax.rem(lane_wide, SLOT)
    own_values = jnp.where(own_block & (depth < HEAD_DIM), 1.0, 0.0)
    own_sum = jnp.where(own_block & (depth == HEAD_DIM), 1.0, 0.0)
    spread = jnp.concatenate(
        [jnp.broadcast_to(q_full[i : i + 1, :], (HEADS, WIDE)) * own_values for i in range(8)], axis=0
    ).astype(jnp.bfloat16)
    same = jnp.concatenate(
        [
            chain_heads * jnp.where(chain_cols == chain_in[0:1, i : i + 1].astype(jnp.float32), 1.0, 0.0)
            for i in range(8)
        ],
        axis=0,
    )
    bias_all[...] = dot(spread, keys.astype(jnp.bfloat16), 1, 0) + same
    values_low[...] = values.astype(jnp.bfloat16)
    own_values_kept[...] = own_values
    own_sum_kept[...] = own_sum
    mask_kept[...] = mask_cols

    r_own.wait()
    others(lambda m: r_copy(m, m).wait_recv())

    def t_copy(m, slot):
        return remote(
            tsend.at[lax.rem(m, 2), lax.div(m, 2)], tin.at[slot], t_send.at[m], t_recv.at[slot],
            lax.div(m, 2), 2 * z + lax.rem(m, 2),
        )

    def t_stays(m):
        return (lax.div(m, 2) == row) & (2 * z + lax.rem(m, 2) == col)

    t_own = pltpu.make_async_copy(tsend.at[col % 2, row], tin.at[me], own_sem.at[5])

    def multiply(step, carry):
        tile = lax.rem(step + z, 2)
        rows = pl.ds(pl.multiple_of(tile * 256, 256), 256)
        sums = []
        for channel in range(2):
            total = jnp.zeros((256, 256), jnp.float32)
            for pair_of_q in range(NQ // 2):
                right = jnp.concatenate(
                    [
                        jnp.concatenate([rbuf[y * NQ + 2 * pair_of_q + n, channel] for y in range(NY)], axis=0)
                        for n in range(2)
                    ],
                    axis=1,
                )
                total = total + dot(lbuf[rows, pair_of_q * 256 : pair_of_q * 256 + 256], right, 1, 1)
            sums.append(total)
        channel = lax.rem(lax.div(lax.broadcasted_iota(jnp.int32, (256, 256), 0), 8), 2)
        both = jnp.where(channel == 0, sums[0], sums[1]).astype(jnp.bfloat16)
        for half in range(2):
            tsend[half, pl.ds(tile * 16, 16)] = both[:, half * 128 : half * 128 + 128].reshape(16, 16, 128)

        def t_start(n, inner):
            m = tile * 32 + lax.rem(me + n, 32)
            stays = t_stays(m)

            @pl.when(stays)
            def _():
                t_own.start()

            @pl.when(jnp.logical_not(stays))
            def _():
                t_copy(m, me).start()

            return inner

        lax.fori_loop(0, 32, t_start, 0)
        return carry

    lax.fori_loop(0, 2, multiply, 0)

    def w_copy(target, slot):
        return remote(wo_msg, wo_all.at[slot], w_send.at[target], w_recv.at[slot], row, target)

    w_own = pltpu.make_async_copy(wo_msg, wo_all.at[col], own_sem.at[3])
    w_own.start()

    def w_start(n, carry):
        w_copy(lax.rem(col + n, NQ), col).start()
        return carry

    lax.fori_loop(1, NQ, w_start, 0)

    others(lambda m: l_copy(m, me).wait_send())
    others(lambda m: r_copy(m, me).wait_send())
    for step in range(4):
        for copy in (z_copy, kz_copy):
            copy(plane_at(-step), 0, up).wait_send()
            if step < 3:
                copy(plane_at(step), 1, down).wait_send()

    def k_sent(n, carry):
        @pl.when(jnp.logical_not(k_to_self(n)))
        def _():
            k_copy(n, k_slot).wait_send()

        return carry

    lax.fori_loop(0, 4, k_sent, 0)

    def t_wait(s, carry):
        from_self = (col // 2 == z) & (s == me)

        @pl.when(from_self)
        def _():
            t_own.wait()

        @pl.when(jnp.logical_not(from_self))
        def _():
            t_copy(s, s).wait_recv()

        return carry

    lax.fori_loop(0, GROUP, t_wait, 0)

    tin32[...] = tin[...].astype(jnp.float32).reshape(1024, 128)

    hidden = w_down.shape[0]

    def pair_step(step, carry):
        rows = pl.ds(pl.multiple_of(step * 256, 256), 256)
        updates = []
        for inner in range(2):
            block = tin32[pl.ds(step * 2 + inner, 128, stride=8), :]
            updates.append(dot(layer_norm(block, 0).astype(jnp.bfloat16), w_out[...], 0, 0))
        update = jnp.concatenate(updates, axis=0)
        pair_mid = pair[rows, :].astype(jnp.float32) + gate_tri[rows, :] * update
        trans_in = layer_norm(pair_mid, -1).astype(jnp.bfloat16)
        both_parts = dot(trans_in, w_in[...], 1, 0)
        gate_part = both_parts[:, :hidden]
        act = (gate_part / (1.0 + jnp.exp(-gate_part)) * both_parts[:, hidden:]).astype(jnp.bfloat16)
        new_pair = (pair_mid + dot(act, w_down[...], 1, 0)).astype(jnp.bfloat16)
        pair_out[rows, :] = new_pair
        bias_norm = layer_norm(new_pair.astype(jnp.float32), -1).astype(jnp.bfloat16)
        linear = dot(bias_weights[...], bias_norm, 1, 1)
        for inner in range(2):
            place = pl.multiple_of(step * 32 + inner * 16, 16)
            bias_all[pl.ds(place, 16), :] += linear[:, inner * 128 : inner * 128 + 128]
        return carry

    lax.fori_loop(0, 4, pair_step, 0)

    weights = jnp.exp(bias_all[...]) * mask_kept[...]
    denominator = jnp.sum(weights, axis=1, keepdims=True)
    products = dot(weights.astype(jnp.bfloat16), values_low[...], 1, 1)
    for i in range(8):
        span = slice(i * HEADS, i * HEADS + HEADS)
        kept = products[span] * own_values_kept[...] + denominator[span] * own_sum_kept[...]
        part[i : i + 1, :] = jnp.sum(kept, axis=0, keepdims=True)

    def p_copy(target, slot):
        return remote(part, parts.at[slot], p_send.at[target], p_recv.at[slot], row, target)

    def p_start(n, carry):
        p_copy(lax.rem(col + n, NQ), col).start()
        return carry

    lax.fori_loop(1, NQ, p_start, 0)
    p_own = pltpu.make_async_copy(part, parts.at[col], own_sem.at[6])
    p_own.start()

    def t_sent(m, carry):
        @pl.when(jnp.logical_not(t_stays(m)))
        def _():
            t_copy(m, me).wait_send()

        return carry

    lax.fori_loop(0, GROUP, t_sent, 0)
    w_own.wait()

    def w_wait(n, carry):
        target = lax.rem(col + n, NQ)
        w_copy(target, target).wait_recv()
        w_copy(target, col).wait_send()
        return carry

    lax.fori_loop(1, NQ, w_wait, 0)
    out_weights = wo_all[...].reshape(WIDE, 384)
    p_own.wait()

    def p_wait(n, carry):
        target = lax.rem(col + n, NQ)
        p_copy(target, target).wait_recv()
        p_copy(target, col).wait_send()
        return carry

    lax.fori_loop(1, NQ, p_wait, 0)
    total = parts[0]
    for n in range(1, NQ):
        total = total + parts[n]
    lane = lax.rem(lax.broadcasted_iota(jnp.int32, (8, WIDE), 1), SLOT)
    below = jnp.where(lane == HEAD_DIM, total, 0.0)
    for shift in (1, 2, 4, 8, 16):
        below = below + pltpu.roll(below, WIDE - shift, 1)
    gated = (gate_full[...] * (total / below)).astype(jnp.bfloat16)
    mixed = dot(gated, out_weights, 1, 0)
    single_out[...] = (single[0:8, :].astype(jnp.float32) + mixed).astype(jnp.bfloat16)


def block(lt, rt, *rest):
    dma = pltpu.SemaphoreType.DMA
    vmem = pl.BlockSpec(memory_space=pltpu.VMEM)
    anywhere = pl.BlockSpec(memory_space=pl.ANY)
    return pl.pallas_call(
        block_kernel,
        out_shape=(
            jax.ShapeDtypeStruct((1024, 128), jnp.bfloat16),
            jax.ShapeDtypeStruct((8, 384), jnp.bfloat16),
        ),
        in_specs=[anywhere] * 2 + [vmem] * 6 + [anywhere] * 6,
        out_specs=(vmem, vmem),
        scratch_shapes=[
            pltpu.VMEM((512, 2048), jnp.bfloat16),
            pltpu.VMEM((GROUP, 2, 64, 128), jnp.bfloat16),
            pltpu.VMEM((2, 32, 16, 128), jnp.bfloat16),
            pltpu.VMEM((GROUP, 16, 128), jnp.bfloat16),
            pltpu.VMEM((1024, 128), jnp.float32),
            pltpu.VMEM((1024, 128), jnp.float32),
            pltpu.VMEM((SLOT, 128), jnp.bfloat16),
            pltpu.VMEM((2 * NQ, SLOT, 128), jnp.bfloat16),
            pltpu.VMEM((8, 128), jnp.float32),
            pltpu.VMEM((NQ, 8, 128), jnp.float32),
            pltpu.VMEM((SLOT, 384), jnp.bfloat16),
            pltpu.VMEM((NQ, SLOT, 384), jnp.bfloat16),
            pltpu.VMEM((128, 384), jnp.float32),
            pltpu.VMEM((128, 128), jnp.float32),
            pltpu.VMEM((8, WIDE), jnp.float32),
            pltpu.VMEM((8, WIDE), jnp.float32),
            pltpu.VMEM((128, 128), jnp.float32),
            pltpu.VMEM((8, WIDE), jnp.float32),
            pltpu.VMEM((NQ, 8, WIDE), jnp.float32),
            pltpu.VMEM((1, 64), jnp.int32),
            pltpu.VMEM((1, 64), jnp.int32),
            pltpu.VMEM((1, HEADS), jnp.float32),
            pltpu.VMEM((HEADS, 128), jnp.bfloat16),
            pltpu.VMEM((4, HEAD_DIM, 384), jnp.bfloat16),
            pltpu.VMEM((HEAD_DIM, 384), jnp.bfloat16),
            pltpu.VMEM((WIDE, 128), jnp.bfloat16),
            pltpu.VMEM((HEADS, WIDE), jnp.float32),
            pltpu.VMEM((HEADS, WIDE), jnp.float32),
            pltpu.VMEM((1, 128), jnp.float32),
            dma((7,)),
            dma((6,)),
            dma((GROUP,)),
            dma((GROUP,)),
            dma((GROUP,)),
            dma((GROUP,)),
            dma((2, NZ)),
            dma((NZ,)),
            dma((4,)),
            dma((4,)),
            dma((2, NZ)),
            dma((NZ,)),
            dma((NQ,)),
            dma((NQ,)),
            dma((NQ,)),
            dma((NQ,)),
            dma((GROUP,)),
            dma((GROUP,)),
            dma((NQ,)),
            dma((NQ,)),
        ],
        compiler_params=pltpu.CompilerParams(
            collective_id=0, has_side_effects=True, vmem_limit_bytes=40 * 1024 * 1024
        ),
        name="pairformer",
    )(lt, rt, *rest)


def local(
    pair,
    panel_left,
    panel_right,
    single,
    token_mask,
    chain_ids,
    w_tri_gate,
    w_tri_out,
    w_trans_in,
    w_trans_down,
    w_bias,
    chain_bias,
    w_attn,
    w_attn_out,
):
    lt = jnp.transpose(panel_left, (2, 0, 1)).reshape(GROUP, 16, 128)
    rt = jnp.transpose(panel_right, (2, 0, 1))
    pair_out, single_out = block(
        lt,
        rt,
        pair.reshape(1024, 128),
        single,
        w_tri_gate,
        w_tri_out,
        w_trans_in,
        w_trans_down,
        token_mask.reshape(1, 64),
        chain_ids.reshape(1, 64),
        chain_bias.reshape(1, HEADS),
        jnp.transpose(w_bias),
        jnp.transpose(w_attn, (0, 2, 1)),
        w_attn_out,
    )
    return (pair_out.reshape(8, 128, 128), single_out)


def solution(mesh):
    in_specs = (
        P("row", "col", None),
        P("row", "col", None),
        P("row", "col", None),
        P("row", None),
        P("row"),
        P("row"),
        P(),
        P(),
        P(),
        P(),
        P(),
        P(),
        P(None, None, "col"),
        P("col", None),
    )
    out_specs = (P("row", "col", None), P("row", None))
    return jax.shard_map(local, mesh=mesh, in_specs=in_specs, out_specs=out_specs, check_vma=False)
```

```python
import jax
import jax.numpy as jnp
from jax import lax
from jax.experimental import pallas as pl
from jax.experimental.pallas import tpu as pltpu
from jax.sharding import PartitionSpec as P

HEAD_DIM = 24
HEADS = 16
NZ = 8
NY = 4
NQ = 16
GROUP = NY * NQ
SLOT = 32
WIDE = HEADS * SLOT
MESH = pl.DeviceIdType.MESH
EARLY = 48
CHUNK = 16
CHUNKS = 4

epsilon = 1e-05


def layer_norm(values, axis):
    mean_val = jnp.mean(values, axis=axis, keepdims=True)
    centred = values - mean_val
    variance = jnp.mean(centred * centred, axis=axis, keepdims=True)
    return centred * lax.rsqrt(variance + epsilon)


def remote(src, dst, send, recv, row, col):
    return pltpu.make_async_remote_copy(
        src_ref=src, dst_ref=dst, send_sem=send, recv_sem=recv, device_id=(row, col), device_id_type=MESH
    )


def dot(a, b, over_a, over_b):
    return lax.dot_general(a, b, (((over_a,), (over_b,)), ((), ())), preferred_element_type=jnp.float32)


def block_kernel(
    left_any, right_any, pair_any, single_any, w_gate_any, w_out_any, w_in_any, w_down_any, mask_any, chain_any, bias_any, w_bias_any, w_attn_any, w_attn_out_any,
    pair_out, single_out,
    left_in, right_in, lt, rt, lbuf, rbuf, tsend, tin, tin32, gate_tri, kv_msg, kv_all, qg_msg, qg_all, wo_msg, wo_all, proj_in, square,
    q_full, gate_full, bias_all, part, parts, mask_in, chain_in, chain_bias, bias_weights, w_attn, w_attn_out,
    values_low, own_values_kept, own_sum_kept, mask_kept,
    pair, single, w_gate, w_out, w_in, w_down,
    own_sem, in_sem, panel_sem, l_send, l_recv, r_send, r_recv, z_send, z_recv, k_send, k_recv, kz_send, kz_recv,
    q_send, q_recv, w_send, w_recv, t_send, t_recv, p_send, p_recv,
):
    row = lax.axis_index("row")
    col = lax.axis_index("col")
    z = row // NY
    yh = row % NY
    me = yh * NQ + col
    up = lax.rem(z + 1, NZ)
    down = lax.rem(z + NZ - 1, NZ)

    def group_device(m):
        return z * NY + lax.div(m, NQ), lax.rem(m, NQ)

    def others(body, start=1, stop=GROUP):
        def step(n, carry):
            body(lax.rem(me + n, GROUP))
            return carry

        lax.fori_loop(start, stop, step, 0)

    barrier = pltpu.get_barrier_semaphore()

    def greet(m):
        pl.semaphore_signal(barrier, inc=1, device_id=group_device(m), device_id_type=MESH)

    left_copy = pltpu.make_async_copy(left_any, left_in, panel_sem.at[CHUNKS])
    left_copy.start()
    single_copy = pltpu.make_async_copy(single_any, single, own_sem.at[7])
    single_copy.start()

    def right_copy(chunk):
        rows = pl.ds(pl.multiple_of(chunk * CHUNK, CHUNK), CHUNK)
        return pltpu.make_async_copy(right_any.at[rows], right_in.at[rows], panel_sem.at[chunk])

    for chunk in range(CHUNKS):
        right_copy(chunk).start()
    for plane in (up, down):
        pl.semaphore_signal(barrier, inc=1, device_id=(plane * NY + yh, col), device_id_type=MESH)
    for n in range(61, GROUP):
        greet(lax.rem(me + n, GROUP))

    home = lax.div(row, 2)
    k_slot = lax.rem(row, 2) * NQ + col
    k_plane = lax.div(k_slot, 4)

    def k_source(n):
        return 2 * col + lax.div(z, 4), 4 * lax.rem(z, 4) + n

    def k_from_self(n):
        source_row, source_col = k_source(n)
        return (source_row == row) & (source_col == col)

    def k_to_self(n):
        return (k_plane == z) & (n == yh) & (home == col)

    def k_greet(n, carry):
        @pl.when(jnp.logical_not(k_from_self(n)))
        def _():
            pl.semaphore_signal(barrier, inc=1, device_id=k_source(n), device_id_type=MESH)

        return carry

    lax.fori_loop(0, 4, k_greet, 0)

    inputs = [
        pltpu.make_async_copy(source, target, in_sem.at[n])
        for n, (source, target) in enumerate(
            (
                (w_attn_any, w_attn), (mask_any, mask_in), (chain_any, chain_in), (bias_any, chain_bias),
                (w_bias_any, bias_weights), (w_attn_out_any, w_attn_out), (w_gate_any, w_gate), (pair_any, pair),
                (w_out_any, w_out), (w_in_any, w_in), (w_down_any, w_down),
            )
        )
    ]
    for copy in inputs:
        copy.start()

    def l_block(m):
        source_row, source_col = group_device(m)
        return lbuf.at[pl.ds(source_row * 16, 16), pl.ds(source_col * 128, 128)]

    def r_block(m):
        return rbuf.at[m]

    def l_copy(m, slot):
        return remote(lt.at[m], l_block(slot), l_send.at[m], l_recv.at[slot], *group_device(m))

    def r_copy(channel, m, slot):
        return remote(
            rt.at[m * 2 + channel], rbuf.at[slot, channel], r_send.at[channel, m], r_recv.at[channel, slot],
            *group_device(m),
        )

    left_copy.wait()
    lt[...] = jnp.transpose(left_in[...].astype(jnp.float32), (2, 0, 1)).reshape(GROUP, 16, 128).astype(jnp.bfloat16)

    def turn(chunk, carry):
        right_copy(chunk).wait()
        for n in range(1, 16):
            if n < 60 // CHUNKS + 1:
                greet(lax.rem(me + chunk * (60 // CHUNKS) + n, GROUP))
        rows = pl.ds(pl.multiple_of(chunk * CHUNK, CHUNK), CHUNK)
        rt[:, rows, :] = jnp.transpose(right_in[rows], (2, 0, 1))
        return carry

    lax.fori_loop(0, CHUNKS, turn, 0)

    l_own = pltpu.make_async_copy(lt.at[me], l_block(me), own_sem.at[0])
    r_own = pltpu.make_async_copy(rt.at[pl.ds(me * 2, 2)], r_block(me), own_sem.at[4])
    l_own.start()
    r_own.start()

    proj_in[...] = jnp.zeros_like(proj_in)
    wo_msg[...] = jnp.zeros_like(wo_msg)
    qg_msg[...] = jnp.zeros_like(qg_msg)
    single_copy.wait()
    single_norm = layer_norm(single[...].astype(jnp.float32), -1).astype(jnp.bfloat16)

    remaining = k_to_self(yh)
    pl.semaphore_wait(barrier, GROUP + 5 - remaining.astype(jnp.int32))
    others(lambda m: r_copy(0, m, me).start(), 1, 9)
    others(lambda m: l_copy(m, me).start())
    others(lambda m: r_copy(0, m, me).start(), 9, EARLY)

    for copy in inputs:
        copy.wait()
    for place, which in enumerate((1, 2, 0, 3)):
        proj_in[place * SLOT : place * SLOT + HEAD_DIM, :] = w_attn[which].astype(jnp.float32)
    proj = proj_in[...].astype(jnp.bfloat16)
    key_value = dot(proj[0 : 2 * SLOT], single_norm, 1, 1)
    square[0:SLOT, 0:64] = key_value[0:SLOT]
    square[0:SLOT, 64:128] = key_value[SLOT : 2 * SLOT]
    square[HEAD_DIM : HEAD_DIM + 1, 0:64] = mask_in[...].astype(jnp.float32)
    square[HEAD_DIM : HEAD_DIM + 1, 64:128] = chain_in[...].astype(jnp.float32)
    kv_msg[...] = square[0:SLOT, :].astype(jnp.bfloat16)
    first_rows = dot(single_norm[0:16], proj[2 * SLOT : 4 * SLOT], 1, 1)[0:8]
    scaled = (first_rows * (HEAD_DIM ** (-0.5))).astype(jnp.bfloat16).astype(jnp.float32)
    lane = lax.broadcasted_iota(jnp.int32, (8, 2 * SLOT), 1)
    qg_msg[:, 0 : 2 * SLOT] = jnp.where(lane < SLOT, scaled, jax.nn.sigmoid(first_rows))

    k_own = pltpu.make_async_copy(kv_msg, kv_all.at[k_slot], own_sem.at[1])

    def k_copy(n, slot):
        return remote(kv_msg, kv_all.at[slot], k_send.at[n], k_recv.at[lax.rem(slot, 4)], k_plane * NY + n, home)

    def k_start(n, carry):
        stays = k_to_self(n)

        @pl.when(stays)
        def _():
            k_own.start()

        @pl.when(jnp.logical_not(stays))
        def _():
            k_copy(n, k_slot).start()

        return carry

    lax.fori_loop(0, 4, k_start, 0)

    def q_copy(target, slot):
        return remote(qg_msg, qg_all.at[slot], q_send.at[target], q_recv.at[slot], row, target)

    q_own = pltpu.make_async_copy(qg_msg, qg_all.at[col], own_sem.at[2])
    q_own.start()

    def q_start(n, carry):
        target = lax.rem(col + n, NQ)
        q_copy(target, col).start()
        return carry

    lax.fori_loop(1, NQ, q_start, 0)
    others(lambda m: r_copy(0, m, me).start(), EARLY, GROUP)
    others(lambda m: r_copy(1, m, me).start())

    proj_in[0:SLOT, :] = jnp.zeros((SLOT, 384), jnp.float32)
    proj_in[0:HEAD_DIM, :] = w_attn_out[...].astype(jnp.float32)
    wo_msg[...] = proj_in[0:SLOT, :].astype(jnp.bfloat16)
    square[...] = jnp.zeros_like(square)
    square[:, 0:HEADS] = jnp.broadcast_to(chain_bias[...], (128, HEADS))
    chain_heads = square[...].T[0:HEADS]

    def gates(tile, carry):
        rows = pl.ds(pl.multiple_of(tile * 256, 256), 256)
        pair_norm = layer_norm(pair[rows, :].astype(jnp.float32), -1).astype(jnp.bfloat16)
        gate_tri[rows, :] = jax.nn.sigmoid(dot(pair_norm, w_gate[...], 1, 0))
        return carry

    lax.fori_loop(0, 4, gates, 0)

    l_own.wait()
    others(lambda m: l_copy(m, m).wait_recv())

    def z_copy(plane, way, target_z):
        block = lbuf.at[pl.ds(plane * 64, 64), :]
        return remote(block, block, z_send.at[way, plane], z_recv.at[plane], target_z * NY + yh, col)

    def kz_copy(plane, way, target_z):
        block = kv_all.at[pl.ds(plane * 4, 4)]
        return remote(block, block, kz_send.at[way, plane], kz_recv.at[plane], target_z * NY + yh, col)

    def plane_at(offset):
        return lax.rem(z + NZ + offset, NZ)

    def ring_step(copy, step):
        if step:
            copy(plane_at(-step), 0, up).wait_recv()
        copy(plane_at(-step), 0, up).start()
        if step < 3:
            if step:
                copy(plane_at(step), 1, down).wait_recv()
            copy(plane_at(step), 1, down).start()

    def ring_end(copy):
        copy(plane_at(4), 0, up).wait_recv()
        copy(plane_at(3), 1, down).wait_recv()

    for step in range(4):
        ring_step(z_copy, step)
    ring_end(z_copy)

    r_own.wait()

    def t_copy(channel, m, slot):
        return remote(
            tsend.at[channel, lax.rem(m, 2), lax.div(m, 2)], tin.at[slot, channel],
            t_send.at[channel, m], t_recv.at[channel, slot], lax.div(m, 2), 2 * z + lax.rem(m, 2),
        )

    def t_stays(m):
        return (lax.div(m, 2) == row) & (2 * z + lax.rem(m, 2) == col)

    def t_own(channel):
        return pltpu.make_async_copy(tsend.at[channel, col % 2, row], tin.at[me, channel], own_sem.at[5 + channel])

    for channel in range(2):
        others(lambda m: r_copy(channel, m, m).wait_recv())

        def multiply(step, carry):
            tile = lax.rem(step + z, 2)
            rows = pl.ds(pl.multiple_of(tile * 256, 256), 256)
            total = jnp.zeros((256, 256), jnp.float32)
            for pair_of_q in range(NQ // 2):
                right = jnp.concatenate(
                    [
                        jnp.concatenate([rbuf[y * NQ + 2 * pair_of_q + n, channel] for y in range(NY)], axis=0)
                        for n in range(2)
                    ],
                    axis=1,
                )
                total = total + dot(lbuf[rows, pair_of_q * 256 : pair_of_q * 256 + 256], right, 1, 1)
            chosen = total.reshape(16, 2, 8, 256)[:, channel].astype(jnp.bfloat16)
            for half in range(2):
                tsend[channel, half, pl.ds(tile * 16, 16)] = chosen[:, :, half * 128 : half * 128 + 128]

            def t_start(n, inner):
                m = tile * 32 + lax.rem(me + n, 32)
                stays = t_stays(m)

                @pl.when(stays)
                def _():
                    t_own(channel).start()

                @pl.when(jnp.logical_not(stays))
                def _():
                    t_copy(channel, m, me).start()

                return inner

            lax.fori_loop(0, 32, t_start, 0)
            return carry

        lax.fori_loop(0, 2, multiply, 0)

    def k_wait(n, carry):
        from_self = k_from_self(n)

        @pl.when(from_self)
        def _():
            k_own.wait()

        @pl.when(jnp.logical_not(from_self))
        def _():
            k_copy(0, z * 4 + n).wait_recv()

        return carry

    lax.fori_loop(0, 4, k_wait, 0)

    ring_step(kz_copy, 0)
    q_own.wait()

    def q_wait(n, carry):
        target = lax.rem(col + n, NQ)
        q_copy(target, col).wait_send()
        q_copy(target, target).wait_recv()
        return carry

    lax.fori_loop(1, NQ, q_wait, 0)
    for head in range(HEADS):
        lanes = slice(head * SLOT, head * SLOT + SLOT)
        q_full[:, lanes] = qg_all[head, :, 0:SLOT]
        gate_full[:, lanes] = qg_all[head, :, SLOT : 2 * SLOT]


    ring_step(kz_copy, 1)

    others(lambda m: l_copy(m, me).wait_send())
    for channel in range(2):
        others(lambda m: r_copy(channel, m, me).wait_send())
    for step in range(4):
        z_copy(plane_at(-step), 0, up).wait_send()
        if step < 3:
            z_copy(plane_at(step), 1, down).wait_send()

    def k_sent(n, carry):
        @pl.when(jnp.logical_not(k_to_self(n)))
        def _():
            k_copy(n, k_slot).wait_send()

        return carry

    lax.fori_loop(0, 4, k_sent, 0)

    ring_step(kz_copy, 2)
    ring_step(kz_copy, 3)
    ring_end(kz_copy)

    low = kv_all[0:HEADS].astype(jnp.float32).reshape(WIDE, 128)
    high = kv_all[HEADS : 2 * HEADS].astype(jnp.float32).reshape(WIDE, 128)
    lane = lax.broadcasted_iota(jnp.int32, (WIDE, 128), 1)
    keys = jnp.where(lane < 64, low, pltpu.roll(high, 64, 1))
    values = jnp.where(lane < 64, pltpu.roll(low, 64, 1), high)
    mask_cols = keys[HEAD_DIM : HEAD_DIM + 1, :]
    chain_cols = values[HEAD_DIM : HEAD_DIM + 1, :]
    head_of_row = lax.broadcasted_iota(jnp.int32, (HEADS, WIDE), 0)
    lane_wide = lax.broadcasted_iota(jnp.int32, (HEADS, WIDE), 1)
    own_block = head_of_row == lax.div(lane_wide, SLOT)
    depth = lax.rem(lane_wide, SLOT)
    own_values = jnp.where(own_block & (depth < HEAD_DIM), 1.0, 0.0)
    own_sum = jnp.where(own_block & (depth == HEAD_DIM), 1.0, 0.0)
    spread = jnp.concatenate(
        [jnp.broadcast_to(q_full[i : i + 1, :], (HEADS, WIDE)) * own_values for i in range(8)], axis=0
    ).astype(jnp.bfloat16)
    same = jnp.concatenate(
        [
            chain_heads * jnp.where(chain_cols == chain_in[0:1, i : i + 1].astype(jnp.float32), 1.0, 0.0)
            for i in range(8)
        ],
        axis=0,
    )
    bias_all[...] = dot(spread, keys.astype(jnp.bfloat16), 1, 0) + same
    values_low[...] = values.astype(jnp.bfloat16)
    own_values_kept[...] = own_values
    own_sum_kept[...] = own_sum
    mask_kept[...] = mask_cols

    for channel in range(2):

        def t_wait(s, carry):
            from_self = (col // 2 == z) & (s == me)

            @pl.when(from_self)
            def _():
                t_own(channel).wait()

            @pl.when(jnp.logical_not(from_self))
            def _():
                t_copy(channel, s, s).wait_recv()

            return carry

        lax.fori_loop(0, GROUP, t_wait, 0)

    tin32[...] = tin[...].astype(jnp.float32).reshape(1024, 128)

    def w_copy(target, slot):
        return remote(wo_msg, wo_all.at[slot], w_send.at[target], w_recv.at[slot], row, target)

    w_own = pltpu.make_async_copy(wo_msg, wo_all.at[col], own_sem.at[3])
    w_own.start()

    hidden = w_down.shape[0]

    def pair_step(step, carry):
        rows = pl.ds(pl.multiple_of(step * 256, 256), 256)
        for n in range(4):
            offset = step * 4 + n

            @pl.when(offset > 0)
            def _():
                w_copy(lax.rem(col + offset, NQ), col).start()

        updates = []
        for inner in range(2):
            block = tin32[pl.ds(step * 2 + inner, 128, stride=8), :]
            updates.append(dot(layer_norm(block, 0).astype(jnp.bfloat16), w_out[...], 0, 0))
        update = jnp.concatenate(updates, axis=0)
        pair_mid = pair[rows, :].astype(jnp.float32) + gate_tri[rows, :] * update
        trans_in = layer_norm(pair_mid, -1).astype(jnp.bfloat16)
        both_parts = dot(trans_in, w_in[...], 1, 0)
        gate_part = both_parts[:, :hidden]
        act = (gate_part / (1.0 + jnp.exp(-gate_part)) * both_parts[:, hidden:]).astype(jnp.bfloat16)
        new_pair = (pair_mid + dot(act, w_down[...], 1, 0)).astype(jnp.bfloat16)
        pair_out[rows, :] = new_pair
        bias_norm = layer_norm(new_pair.astype(jnp.float32), -1).astype(jnp.bfloat16)
        linear = dot(bias_weights[...], bias_norm, 1, 1)
        for inner in range(2):
            place = pl.multiple_of(step * 32 + inner * 16, 16)
            bias_all[pl.ds(place, 16), :] += linear[:, inner * 128 : inner * 128 + 128]
        return carry

    lax.fori_loop(0, 4, pair_step, 0)

    weights = jnp.exp(bias_all[...]) * mask_kept[...]
    denominator = jnp.sum(weights, axis=1, keepdims=True)
    products = dot(weights.astype(jnp.bfloat16), values_low[...], 1, 1)
    for i in range(8):
        span = slice(i * HEADS, i * HEADS + HEADS)
        kept = products[span] * own_values_kept[...] + denominator[span] * own_sum_kept[...]
        part[i : i + 1, :] = jnp.sum(kept, axis=0, keepdims=True)

    def p_copy(target, slot):
        return remote(part, parts.at[slot], p_send.at[target], p_recv.at[slot], row, target)

    def p_start(n, carry):
        p_copy(lax.rem(col + n, NQ), col).start()
        return carry

    lax.fori_loop(1, NQ, p_start, 0)
    p_own = pltpu.make_async_copy(part, parts.at[col], own_sem.at[8])
    p_own.start()

    for step in range(4):
        kz_copy(plane_at(-step), 0, up).wait_send()
        if step < 3:
            kz_copy(plane_at(step), 1, down).wait_send()

    def t_sent(m, carry):
        @pl.when(jnp.logical_not(t_stays(m)))
        def _():
            for channel in range(2):
                t_copy(channel, m, me).wait_send()

        return carry

    lax.fori_loop(0, GROUP, t_sent, 0)
    w_own.wait()

    def w_wait(n, carry):
        target = lax.rem(col + n, NQ)
        w_copy(target, target).wait_recv()
        w_copy(target, col).wait_send()
        return carry

    lax.fori_loop(1, NQ, w_wait, 0)
    out_weights = wo_all[...].reshape(WIDE, 384)
    p_own.wait()

    def p_wait(n, carry):
        target = lax.rem(col + n, NQ)
        p_copy(target, target).wait_recv()
        p_copy(target, col).wait_send()
        return carry

    lax.fori_loop(1, NQ, p_wait, 0)
    total = parts[0]
    for n in range(1, NQ):
        total = total + parts[n]
    lane = lax.rem(lax.broadcasted_iota(jnp.int32, (8, WIDE), 1), SLOT)
    below = jnp.where(lane == HEAD_DIM, total, 0.0)
    for shift in (1, 2, 4, 8, 16):
        below = below + pltpu.roll(below, WIDE - shift, 1)
    gated = (gate_full[...] * (total / below)).astype(jnp.bfloat16)
    mixed = dot(gated, out_weights, 1, 0)
    single_out[...] = (single[0:8, :].astype(jnp.float32) + mixed).astype(jnp.bfloat16)


def block(*operands):
    dma = pltpu.SemaphoreType.DMA
    vmem = pl.BlockSpec(memory_space=pltpu.VMEM)
    anywhere = pl.BlockSpec(memory_space=pl.ANY)
    return pl.pallas_call(
        block_kernel,
        out_shape=(
            jax.ShapeDtypeStruct((1024, 128), jnp.bfloat16),
            jax.ShapeDtypeStruct((8, 384), jnp.bfloat16),
        ),
        in_specs=[anywhere] * 14,
        out_specs=(vmem, vmem),
        scratch_shapes=[
            pltpu.VMEM((8, 128, 128), jnp.bfloat16),
            pltpu.VMEM((64, 128, 128), jnp.bfloat16),
            pltpu.VMEM((GROUP, 16, 128), jnp.bfloat16),
            pltpu.VMEM((128, 64, 128), jnp.bfloat16),
            pltpu.VMEM((512, 2048), jnp.bfloat16),
            pltpu.VMEM((GROUP, 2, 64, 128), jnp.bfloat16),
            pltpu.VMEM((2, 2, 32, 8, 128), jnp.bfloat16),
            pltpu.VMEM((GROUP, 2, 8, 128), jnp.bfloat16),
            pltpu.VMEM((1024, 128), jnp.float32),
            pltpu.VMEM((1024, 128), jnp.float32),
            pltpu.VMEM((SLOT, 128), jnp.bfloat16),
            pltpu.VMEM((2 * NQ, SLOT, 128), jnp.bfloat16),
            pltpu.VMEM((8, 128), jnp.float32),
            pltpu.VMEM((NQ, 8, 128), jnp.float32),
            pltpu.VMEM((SLOT, 384), jnp.bfloat16),
            pltpu.VMEM((NQ, SLOT, 384), jnp.bfloat16),
            pltpu.VMEM((128, 384), jnp.float32),
            pltpu.VMEM((128, 128), jnp.float32),
            pltpu.VMEM((8, WIDE), jnp.float32),
            pltpu.VMEM((8, WIDE), jnp.float32),
            pltpu.VMEM((128, 128), jnp.float32),
            pltpu.VMEM((8, WIDE), jnp.float32),
            pltpu.VMEM((NQ, 8, WIDE), jnp.float32),
            pltpu.VMEM((1, 64), jnp.int32),
            pltpu.VMEM((1, 64), jnp.int32),
            pltpu.VMEM((1, HEADS), jnp.float32),
            pltpu.VMEM((HEADS, 128), jnp.bfloat16),
            pltpu.VMEM((4, HEAD_DIM, 384), jnp.bfloat16),
            pltpu.VMEM((HEAD_DIM, 384), jnp.bfloat16),
            pltpu.VMEM((WIDE, 128), jnp.bfloat16),
            pltpu.VMEM((HEADS, WIDE), jnp.float32),
            pltpu.VMEM((HEADS, WIDE), jnp.float32),
            pltpu.VMEM((1, 128), jnp.float32),
            pltpu.VMEM((1024, 128), jnp.bfloat16),
            pltpu.VMEM((64, 384), jnp.bfloat16),
            pltpu.VMEM((128, 128), jnp.bfloat16),
            pltpu.VMEM((128, 128), jnp.bfloat16),
            pltpu.VMEM((128, 1024), jnp.bfloat16),
            pltpu.VMEM((512, 128), jnp.bfloat16),
            dma((9,)),
            dma((11,)),
            dma((CHUNKS + 1,)),
            dma((GROUP,)),
            dma((GROUP,)),
            dma((2, GROUP)),
            dma((2, GROUP)),
            dma((2, NZ)),
            dma((NZ,)),
            dma((4,)),
            dma((4,)),
            dma((2, NZ)),
            dma((NZ,)),
            dma((NQ,)),
            dma((NQ,)),
            dma((NQ,)),
            dma((NQ,)),
            dma((2, GROUP)),
            dma((2, GROUP)),
            dma((NQ,)),
            dma((NQ,)),
        ],
        compiler_params=pltpu.CompilerParams(
            collective_id=0, has_side_effects=True, vmem_limit_bytes=60 * 1024 * 1024
        ),
        name="pairformer",
    )(*operands)


def local(
    pair,
    panel_left,
    panel_right,
    single,
    token_mask,
    chain_ids,
    w_tri_gate,
    w_tri_out,
    w_trans_in,
    w_trans_down,
    w_bias,
    chain_bias,
    w_attn,
    w_attn_out,
):
    pair_out, single_out = block(
        panel_left,
        panel_right,
        pair.reshape(1024, 128),
        single,
        w_tri_gate,
        w_tri_out,
        w_trans_in,
        w_trans_down,
        token_mask.reshape(1, 64),
        chain_ids.reshape(1, 64),
        chain_bias.reshape(1, HEADS),
        jnp.transpose(w_bias),
        jnp.transpose(w_attn, (0, 2, 1)),
        w_attn_out,
    )
    return (pair_out.reshape(8, 128, 128), single_out)


def solution(mesh):
    in_specs = (
        P("row", "col", None),
        P("row", "col", None),
        P("row", "col", None),
        P("row", None),
        P("row"),
        P("row"),
        P(),
        P(),
        P(),
        P(),
        P(),
        P(),
        P(None, None, "col"),
        P("col", None),
    )
    out_specs = (P("row", "col", None), P("row", None))
    return jax.shard_map(local, mesh=mesh, in_specs=in_specs, out_specs=out_specs, check_vma=False)
```

```python
import jax
import jax.numpy as jnp
from jax import lax
from jax.experimental import pallas as pl
from jax.experimental.pallas import tpu as pltpu
from jax.sharding import PartitionSpec as P

HEAD_DIM = 24
HEADS = 16
NZ = 8
NY = 4
NQ = 16
GROUP = NY * NQ
SLOT = 32
WIDE = HEADS * SLOT
MESH = pl.DeviceIdType.MESH
EARLY = 48
CHUNK = 16
CHUNKS = 4

epsilon = 1e-05


def layer_norm(values, axis):
    mean_val = jnp.mean(values, axis=axis, keepdims=True)
    centred = values - mean_val
    variance = jnp.mean(centred * centred, axis=axis, keepdims=True)
    return centred * lax.rsqrt(variance + epsilon)


def remote(src, dst, send, recv, row, col):
    return pltpu.make_async_remote_copy(
        src_ref=src, dst_ref=dst, send_sem=send, recv_sem=recv, device_id=(row, col), device_id_type=MESH
    )


def dot(a, b, over_a, over_b):
    return lax.dot_general(a, b, (((over_a,), (over_b,)), ((), ())), preferred_element_type=jnp.float32)


def block_kernel(
    left_any, right_any, pair_any, single_any, w_gate_any, w_out_any, w_in_any, w_down_any, mask_any, chain_any, bias_any, w_bias_any, w_attn_any, w_attn_out_any,
    pair_out, single_out,
    left_in, right_in, lt, rt, lbuf, rbuf, tsend, tin, tin32, gate_tri, kv_msg, kv_all, qg_msg, qg_all, wo_msg, wo_all, proj_in, square,
    q_full, gate_full, bias_all, part, parts, mask_in, chain_in, chain_bias, bias_weights, w_attn, w_attn_out,
    values_low, own_values_kept, own_sum_kept, mask_kept,
    pair, single, w_gate, w_out, w_in, w_down,
    own_sem, in_sem, panel_sem, l_send, l_recv, r_send, r_recv, z_send, z_recv, k_send, k_recv, kz_send, kz_recv,
    q_send, q_recv, w_send, w_recv, t_send, t_recv, p_send, p_recv,
):
    row = lax.axis_index("row")
    col = lax.axis_index("col")
    z = row // NY
    yh = row % NY
    me = yh * NQ + col
    up = lax.rem(z + 1, NZ)
    down = lax.rem(z + NZ - 1, NZ)

    def group_device(m):
        return z * NY + lax.div(m, NQ), lax.rem(m, NQ)

    def others(body, start=1, stop=GROUP):
        def step(n, carry):
            body(lax.rem(me + n, GROUP))
            return carry

        lax.fori_loop(start, stop, step, 0)

    barrier = pltpu.get_barrier_semaphore()

    def greet(m):
        pl.semaphore_signal(barrier, inc=1, device_id=group_device(m), device_id_type=MESH)

    left_copy = pltpu.make_async_copy(left_any, left_in, panel_sem.at[CHUNKS])
    left_copy.start()
    single_copy = pltpu.make_async_copy(single_any, single, own_sem.at[7])
    single_copy.start()

    def right_copy(chunk):
        rows = pl.ds(pl.multiple_of(chunk * CHUNK, CHUNK), CHUNK)
        return pltpu.make_async_copy(right_any.at[rows], right_in.at[rows], panel_sem.at[chunk])

    for chunk in range(CHUNKS):
        right_copy(chunk).start()
    for plane in (up, down):
        pl.semaphore_signal(barrier, inc=1, device_id=(plane * NY + yh, col), device_id_type=MESH)
    for n in range(61, GROUP):
        greet(lax.rem(me + n, GROUP))

    home = lax.div(row, 2)
    k_slot = lax.rem(row, 2) * NQ + col
    k_plane = lax.div(k_slot, 4)

    def k_source(n):
        return 2 * col + lax.div(z, 4), 4 * lax.rem(z, 4) + n

    def k_from_self(n):
        source_row, source_col = k_source(n)
        return (source_row == row) & (source_col == col)

    def k_to_self(n):
        return (k_plane == z) & (n == yh) & (home == col)

    def k_greet(n, carry):
        @pl.when(jnp.logical_not(k_from_self(n)))
        def _():
            pl.semaphore_signal(barrier, inc=1, device_id=k_source(n), device_id_type=MESH)

        return carry

    lax.fori_loop(0, 4, k_greet, 0)

    inputs = [
        pltpu.make_async_copy(source, target, in_sem.at[n])
        for n, (source, target) in enumerate(
            (
                (w_attn_any, w_attn), (mask_any, mask_in), (chain_any, chain_in), (bias_any, chain_bias),
                (w_bias_any, bias_weights), (w_attn_out_any, w_attn_out), (w_gate_any, w_gate), (pair_any, pair),
                (w_out_any, w_out), (w_in_any, w_in), (w_down_any, w_down),
            )
        )
    ]
    for copy in inputs:
        copy.start()

    def l_block(m):
        source_row, source_col = group_device(m)
        return lbuf.at[pl.ds(source_row * 16, 16), pl.ds(source_col * 128, 128)]

    def r_block(m):
        return rbuf.at[m]

    def l_copy(m, slot):
        return remote(lt.at[m], l_block(slot), l_send, l_recv.at[slot], *group_device(m))

    def r_copy(channel, m, slot):
        return remote(
            rt.at[m * 2 + channel], rbuf.at[slot, channel], r_send, r_recv.at[channel, slot],
            *group_device(m),
        )

    left_copy.wait()
    lt[...] = jnp.transpose(left_in[...].astype(jnp.float32), (2, 0, 1)).reshape(GROUP, 16, 128).astype(jnp.bfloat16)

    def turn(chunk, carry):
        right_copy(chunk).wait()
        for n in range(1, 16):
            if n < 60 // CHUNKS + 1:
                greet(lax.rem(me + chunk * (60 // CHUNKS) + n, GROUP))
        rows = pl.ds(pl.multiple_of(chunk * CHUNK, CHUNK), CHUNK)
        rt[:, rows, :] = jnp.transpose(right_in[rows], (2, 0, 1))
        return carry

    lax.fori_loop(0, CHUNKS, turn, 0)

    l_own = pltpu.make_async_copy(lt.at[me], l_block(me), own_sem.at[0])
    r_own = pltpu.make_async_copy(rt.at[pl.ds(me * 2, 2)], r_block(me), own_sem.at[4])
    l_own.start()
    r_own.start()

    proj_in[...] = jnp.zeros_like(proj_in)
    wo_msg[...] = jnp.zeros_like(wo_msg)
    qg_msg[...] = jnp.zeros_like(qg_msg)
    single_copy.wait()
    single_norm = layer_norm(single[...].astype(jnp.float32), -1).astype(jnp.bfloat16)

    remaining = k_to_self(yh)
    pl.semaphore_wait(barrier, GROUP + 5 - remaining.astype(jnp.int32))
    others(lambda m: r_copy(0, m, me).start(), 1, 9)
    others(lambda m: l_copy(m, me).start())
    others(lambda m: r_copy(0, m, me).start(), 9, EARLY)

    for copy in inputs:
        copy.wait()
    for place, which in enumerate((1, 2, 0, 3)):
        proj_in[place * SLOT : place * SLOT + HEAD_DIM, :] = w_attn[which].astype(jnp.float32)
    proj = proj_in[...].astype(jnp.bfloat16)
    key_value = dot(proj[0 : 2 * SLOT], single_norm, 1, 1)
    square[0:SLOT, 0:64] = key_value[0:SLOT]
    square[0:SLOT, 64:128] = key_value[SLOT : 2 * SLOT]
    square[HEAD_DIM : HEAD_DIM + 1, 0:64] = mask_in[...].astype(jnp.float32)
    square[HEAD_DIM : HEAD_DIM + 1, 64:128] = chain_in[...].astype(jnp.float32)
    kv_msg[...] = square[0:SLOT, :].astype(jnp.bfloat16)
    first_rows = dot(single_norm[0:16], proj[2 * SLOT : 4 * SLOT], 1, 1)[0:8]
    scaled = (first_rows * (HEAD_DIM ** (-0.5))).astype(jnp.bfloat16).astype(jnp.float32)
    lane = lax.broadcasted_iota(jnp.int32, (8, 2 * SLOT), 1)
    qg_msg[:, 0 : 2 * SLOT] = jnp.where(lane < SLOT, scaled, jax.nn.sigmoid(first_rows))

    k_own = pltpu.make_async_copy(kv_msg, kv_all.at[k_slot], own_sem.at[1])

    def k_copy(n, slot):
        return remote(kv_msg, kv_all.at[slot], k_send.at[n], k_recv.at[lax.rem(slot, 4)], k_plane * NY + n, home)

    def k_start(n, carry):
        stays = k_to_self(n)

        @pl.when(stays)
        def _():
            k_own.start()

        @pl.when(jnp.logical_not(stays))
        def _():
            k_copy(n, k_slot).start()

        return carry

    lax.fori_loop(0, 4, k_start, 0)

    def q_copy(target, slot):
        return remote(qg_msg, qg_all.at[slot], q_send.at[target], q_recv.at[slot], row, target)

    q_own = pltpu.make_async_copy(qg_msg, qg_all.at[col], own_sem.at[2])
    q_own.start()

    def q_start(n, carry):
        target = lax.rem(col + n, NQ)
        q_copy(target, col).start()
        return carry

    lax.fori_loop(1, NQ, q_start, 0)
    others(lambda m: r_copy(0, m, me).start(), EARLY, GROUP)
    others(lambda m: r_copy(1, m, me).start())

    proj_in[0:SLOT, :] = jnp.zeros((SLOT, 384), jnp.float32)
    proj_in[0:HEAD_DIM, :] = w_attn_out[...].astype(jnp.float32)
    wo_msg[...] = proj_in[0:SLOT, :].astype(jnp.bfloat16)
    square[...] = jnp.zeros_like(square)
    square[:, 0:HEADS] = jnp.broadcast_to(chain_bias[...], (128, HEADS))
    chain_heads = square[...].T[0:HEADS]

    def gates(tile, carry):
        rows = pl.ds(pl.multiple_of(tile * 256, 256), 256)
        pair_norm = layer_norm(pair[rows, :].astype(jnp.float32), -1).astype(jnp.bfloat16)
        gate_tri[rows, :] = jax.nn.sigmoid(dot(pair_norm, w_gate[...], 1, 0))
        return carry

    lax.fori_loop(0, 4, gates, 0)

    l_own.wait()
    others(lambda m: l_copy(m, m).wait_recv())

    def z_copy(plane, way, target_z):
        block = lbuf.at[pl.ds(plane * 64, 64), :]
        return remote(block, block, z_send.at[way, plane], z_recv.at[plane], target_z * NY + yh, col)

    def kz_copy(plane, way, target_z):
        block = kv_all.at[pl.ds(plane * 4, 4)]
        return remote(block, block, kz_send.at[way, plane], kz_recv.at[plane], target_z * NY + yh, col)

    def plane_at(offset):
        return lax.rem(z + NZ + offset, NZ)

    def ring_step(copy, step):
        if step:
            copy(plane_at(-step), 0, up).wait_recv()
        copy(plane_at(-step), 0, up).start()
        if step < 3:
            if step:
                copy(plane_at(step), 1, down).wait_recv()
            copy(plane_at(step), 1, down).start()

    def ring_end(copy):
        copy(plane_at(4), 0, up).wait_recv()
        copy(plane_at(3), 1, down).wait_recv()

    for step in range(4):
        ring_step(z_copy, step)
    ring_end(z_copy)

    def k_wait(n, carry):
        from_self = k_from_self(n)

        @pl.when(from_self)
        def _():
            k_own.wait()

        @pl.when(jnp.logical_not(from_self))
        def _():
            k_copy(0, z * 4 + n).wait_recv()

        return carry

    lax.fori_loop(0, 4, k_wait, 0)

    ring_step(kz_copy, 0)
    r_own.wait()

    def t_copy(channel, m, slot):
        return remote(
            tsend.at[channel, lax.rem(m, 2), lax.div(m, 2)], tin.at[slot, channel],
            t_send, t_recv.at[channel, slot], lax.div(m, 2), 2 * z + lax.rem(m, 2),
        )

    def t_stays(m):
        return (lax.div(m, 2) == row) & (2 * z + lax.rem(m, 2) == col)

    def t_own(channel):
        return pltpu.make_async_copy(tsend.at[channel, col % 2, row], tin.at[me, channel], own_sem.at[5 + channel])

    for channel in range(2):
        others(lambda m: r_copy(channel, m, m).wait_recv())

        def multiply(step, carry):
            tile = lax.rem(step + z, 2)
            rows = pl.ds(pl.multiple_of(tile * 256, 256), 256)
            total = jnp.zeros((256, 256), jnp.float32)
            for pair_of_q in range(NQ // 2):
                right = jnp.concatenate(
                    [
                        jnp.concatenate([rbuf[y * NQ + 2 * pair_of_q + n, channel] for y in range(NY)], axis=0)
                        for n in range(2)
                    ],
                    axis=1,
                )
                total = total + dot(lbuf[rows, pair_of_q * 256 : pair_of_q * 256 + 256], right, 1, 1)
            chosen = total.reshape(16, 2, 8, 256)[:, channel].astype(jnp.bfloat16)
            for half in range(2):
                tsend[channel, half, pl.ds(tile * 16, 16)] = chosen[:, :, half * 128 : half * 128 + 128]

            def t_start(n, inner):
                m = tile * 32 + lax.rem(me + n, 32)
                stays = t_stays(m)

                @pl.when(stays)
                def _():
                    t_own(channel).start()

                @pl.when(jnp.logical_not(stays))
                def _():
                    t_copy(channel, m, me).start()

                return inner

            lax.fori_loop(0, 32, t_start, 0)
            return carry

        lax.fori_loop(0, 2, multiply, 0)
        if channel == 0:
            ring_step(kz_copy, 1)
            q_own.wait()

            def q_wait(n, carry):
                target = lax.rem(col + n, NQ)
                q_copy(target, col).wait_send()
                q_copy(target, target).wait_recv()
                return carry

            lax.fori_loop(1, NQ, q_wait, 0)
            for head in range(HEADS):
                lanes = slice(head * SLOT, head * SLOT + SLOT)
                q_full[:, lanes] = qg_all[head, :, 0:SLOT]
                gate_full[:, lanes] = qg_all[head, :, SLOT : 2 * SLOT]
            ring_step(kz_copy, 2)

    ring_step(kz_copy, 3)
    ring_end(kz_copy)

    low = kv_all[0:HEADS].astype(jnp.float32).reshape(WIDE, 128)
    high = kv_all[HEADS : 2 * HEADS].astype(jnp.float32).reshape(WIDE, 128)
    lane = lax.broadcasted_iota(jnp.int32, (WIDE, 128), 1)
    keys = jnp.where(lane < 64, low, pltpu.roll(high, 64, 1))
    values = jnp.where(lane < 64, pltpu.roll(low, 64, 1), high)
    mask_cols = keys[HEAD_DIM : HEAD_DIM + 1, :]
    chain_cols = values[HEAD_DIM : HEAD_DIM + 1, :]
    head_of_row = lax.broadcasted_iota(jnp.int32, (HEADS, WIDE), 0)
    lane_wide = lax.broadcasted_iota(jnp.int32, (HEADS, WIDE), 1)
    own_block = head_of_row == lax.div(lane_wide, SLOT)
    depth = lax.rem(lane_wide, SLOT)
    own_values = jnp.where(own_block & (depth < HEAD_DIM), 1.0, 0.0)
    own_sum = jnp.where(own_block & (depth == HEAD_DIM), 1.0, 0.0)
    spread = jnp.concatenate(
        [jnp.broadcast_to(q_full[i : i + 1, :], (HEADS, WIDE)) * own_values for i in range(8)], axis=0
    ).astype(jnp.bfloat16)
    same = jnp.concatenate(
        [
            chain_heads * jnp.where(chain_cols == chain_in[0:1, i : i + 1].astype(jnp.float32), 1.0, 0.0)
            for i in range(8)
        ],
        axis=0,
    )
    bias_all[...] = dot(spread, keys.astype(jnp.bfloat16), 1, 0) + same
    values_low[...] = values.astype(jnp.bfloat16)
    own_values_kept[...] = own_values
    own_sum_kept[...] = own_sum
    mask_kept[...] = mask_cols

    for channel in range(2):

        def t_wait(s, carry):
            from_self = (col // 2 == z) & (s == me)

            @pl.when(from_self)
            def _():
                t_own(channel).wait()

            @pl.when(jnp.logical_not(from_self))
            def _():
                t_copy(channel, s, s).wait_recv()

            return carry

        lax.fori_loop(0, GROUP, t_wait, 0)

    tin32[...] = tin[...].astype(jnp.float32).reshape(1024, 128)

    def w_copy(target, slot):
        return remote(wo_msg, wo_all.at[slot], w_send.at[target], w_recv.at[slot], row, target)

    w_own = pltpu.make_async_copy(wo_msg, wo_all.at[col], own_sem.at[3])
    w_own.start()

    hidden = w_down.shape[0]

    def pair_step(step, carry):
        rows = pl.ds(pl.multiple_of(step * 256, 256), 256)
        for n in range(4):
            offset = step * 4 + n

            @pl.when(offset > 0)
            def _():
                w_copy(lax.rem(col + offset, NQ), col).start()

        updates = []
        for inner in range(2):
            block = tin32[pl.ds(step * 2 + inner, 128, stride=8), :]
            updates.append(dot(layer_norm(block, 0).astype(jnp.bfloat16), w_out[...], 0, 0))
        update = jnp.concatenate(updates, axis=0)
        pair_mid = pair[rows, :].astype(jnp.float32) + gate_tri[rows, :] * update
        trans_in = layer_norm(pair_mid, -1).astype(jnp.bfloat16)
        both_parts = dot(trans_in, w_in[...], 1, 0)
        gate_part = both_parts[:, :hidden]
        act = (gate_part / (1.0 + jnp.exp(-gate_part)) * both_parts[:, hidden:]).astype(jnp.bfloat16)
        new_pair = (pair_mid + dot(act, w_down[...], 1, 0)).astype(jnp.bfloat16)
        pair_out[rows, :] = new_pair
        bias_norm = layer_norm(new_pair.astype(jnp.float32), -1).astype(jnp.bfloat16)
        linear = dot(bias_weights[...], bias_norm, 1, 1)
        for inner in range(2):
            place = pl.multiple_of(step * 32 + inner * 16, 16)
            bias_all[pl.ds(place, 16), :] += linear[:, inner * 128 : inner * 128 + 128]
        return carry

    lax.fori_loop(0, 4, pair_step, 0)

    weights = jnp.exp(bias_all[...]) * mask_kept[...]
    denominator = jnp.sum(weights, axis=1, keepdims=True)
    products = dot(weights.astype(jnp.bfloat16), values_low[...], 1, 1)
    for i in range(8):
        span = slice(i * HEADS, i * HEADS + HEADS)
        kept = products[span] * own_values_kept[...] + denominator[span] * own_sum_kept[...]
        part[i : i + 1, :] = jnp.sum(kept, axis=0, keepdims=True)

    def p_copy(target, slot):
        return remote(part, parts.at[slot], p_send.at[target], p_recv.at[slot], row, target)

    def p_start(n, carry):
        p_copy(lax.rem(col + n, NQ), col).start()
        return carry

    lax.fori_loop(1, NQ, p_start, 0)
    p_own = pltpu.make_async_copy(part, parts.at[col], own_sem.at[8])
    p_own.start()

    for step in range(4):
        kz_copy(plane_at(-step), 0, up).wait_send()
        if step < 3:
            kz_copy(plane_at(step), 1, down).wait_send()

    def sent(ref, sem):
        remote(ref, ref, sem, own_sem.at[9], up * NY + yh, col).wait_send()

    sent(lt.at[pl.ds(0, GROUP - 1)], l_send)
    sent(rt.at[pl.ds(0, 2 * GROUP - 2)], r_send)
    keeps_one = lax.div(col, 2) == z

    @pl.when(keeps_one)
    def _():
        sent(tin.at[pl.ds(0, GROUP - 1)], t_send)

    @pl.when(jnp.logical_not(keeps_one))
    def _():
        sent(tin, t_send)

    for step in range(4):
        z_copy(plane_at(-step), 0, up).wait_send()
        if step < 3:
            z_copy(plane_at(step), 1, down).wait_send()

    def k_sent(n, carry):
        @pl.when(jnp.logical_not(k_to_self(n)))
        def _():
            k_copy(n, k_slot).wait_send()

        return carry

    lax.fori_loop(0, 4, k_sent, 0)

    w_own.wait()

    def w_wait(n, carry):
        target = lax.rem(col + n, NQ)
        w_copy(target, target).wait_recv()
        w_copy(target, col).wait_send()
        return carry

    lax.fori_loop(1, NQ, w_wait, 0)
    out_weights = wo_all[...].reshape(WIDE, 384)
    p_own.wait()

    def p_wait(n, carry):
        target = lax.rem(col + n, NQ)
        p_copy(target, target).wait_recv()
        p_copy(target, col).wait_send()
        return carry

    lax.fori_loop(1, NQ, p_wait, 0)
    total = parts[0]
    for n in range(1, NQ):
        total = total + parts[n]
    lane = lax.rem(lax.broadcasted_iota(jnp.int32, (8, WIDE), 1), SLOT)
    below = jnp.where(lane == HEAD_DIM, total, 0.0)
    for shift in (1, 2, 4, 8, 16):
        below = below + pltpu.roll(below, WIDE - shift, 1)
    gated = (gate_full[...] * (total / below)).astype(jnp.bfloat16)
    mixed = dot(gated, out_weights, 1, 0)
    single_out[...] = (single[0:8, :].astype(jnp.float32) + mixed).astype(jnp.bfloat16)


def block(*operands):
    dma = pltpu.SemaphoreType.DMA
    vmem = pl.BlockSpec(memory_space=pltpu.VMEM)
    anywhere = pl.BlockSpec(memory_space=pltpu.HBM)
    return pl.pallas_call(
        block_kernel,
        out_shape=(
            jax.ShapeDtypeStruct((1024, 128), jnp.bfloat16),
            jax.ShapeDtypeStruct((8, 384), jnp.bfloat16),
        ),
        in_specs=[anywhere] * 14,
        out_specs=(vmem, vmem),
        scratch_shapes=[
            pltpu.VMEM((8, 128, 128), jnp.bfloat16),
            pltpu.VMEM((64, 128, 128), jnp.bfloat16),
            pltpu.VMEM((GROUP, 16, 128), jnp.bfloat16),
            pltpu.VMEM((128, 64, 128), jnp.bfloat16),
            pltpu.VMEM((512, 2048), jnp.bfloat16),
            pltpu.VMEM((GROUP, 2, 64, 128), jnp.bfloat16),
            pltpu.VMEM((2, 2, 32, 8, 128), jnp.bfloat16),
            pltpu.VMEM((GROUP, 2, 8, 128), jnp.bfloat16),
            pltpu.VMEM((1024, 128), jnp.float32),
            pltpu.VMEM((1024, 128), jnp.float32),
            pltpu.VMEM((SLOT, 128), jnp.bfloat16),
            pltpu.VMEM((2 * NQ, SLOT, 128), jnp.bfloat16),
            pltpu.VMEM((8, 128), jnp.float32),
            pltpu.VMEM((NQ, 8, 128), jnp.float32),
            pltpu.VMEM((SLOT, 384), jnp.bfloat16),
            pltpu.VMEM((NQ, SLOT, 384), jnp.bfloat16),
            pltpu.VMEM((128, 384), jnp.float32),
            pltpu.VMEM((128, 128), jnp.float32),
            pltpu.VMEM((8, WIDE), jnp.float32),
            pltpu.VMEM((8, WIDE), jnp.float32),
            pltpu.VMEM((128, 128), jnp.float32),
            pltpu.VMEM((8, WIDE), jnp.float32),
            pltpu.VMEM((NQ, 8, WIDE), jnp.float32),
            pltpu.VMEM((1, 64), jnp.int32),
            pltpu.VMEM((1, 64), jnp.int32),
            pltpu.VMEM((1, HEADS), jnp.float32),
            pltpu.VMEM((HEADS, 128), jnp.bfloat16),
            pltpu.VMEM((4, HEAD_DIM, 384), jnp.bfloat16),
            pltpu.VMEM((HEAD_DIM, 384), jnp.bfloat16),
            pltpu.VMEM((WIDE, 128), jnp.bfloat16),
            pltpu.VMEM((HEADS, WIDE), jnp.float32),
            pltpu.VMEM((HEADS, WIDE), jnp.float32),
            pltpu.VMEM((1, 128), jnp.float32),
            pltpu.VMEM((1024, 128), jnp.bfloat16),
            pltpu.VMEM((64, 384), jnp.bfloat16),
            pltpu.VMEM((128, 128), jnp.bfloat16),
            pltpu.VMEM((128, 128), jnp.bfloat16),
            pltpu.VMEM((128, 1024), jnp.bfloat16),
            pltpu.VMEM((512, 128), jnp.bfloat16),
            dma((10,)),
            dma((11,)),
            dma((CHUNKS + 1,)),
            dma,
            dma((GROUP,)),
            dma,
            dma((2, GROUP)),
            dma((2, NZ)),
            dma((NZ,)),
            dma((4,)),
            dma((4,)),
            dma((2, NZ)),
            dma((NZ,)),
            dma((NQ,)),
            dma((NQ,)),
            dma((NQ,)),
            dma((NQ,)),
            dma,
            dma((2, GROUP)),
            dma((NQ,)),
            dma((NQ,)),
        ],
        compiler_params=pltpu.CompilerParams(
            collective_id=0, has_side_effects=True, vmem_limit_bytes=58 * 1024 * 1024
        ),
        name="pairformer",
    )(*operands)


def local(
    pair,
    panel_left,
    panel_right,
    single,
    token_mask,
    chain_ids,
    w_tri_gate,
    w_tri_out,
    w_trans_in,
    w_trans_down,
    w_bias,
    chain_bias,
    w_attn,
    w_attn_out,
):
    pair_out, single_out = block(
        panel_left,
        panel_right,
        pair.reshape(1024, 128),
        single,
        w_tri_gate,
        w_tri_out,
        w_trans_in,
        w_trans_down,
        token_mask.reshape(1, 64),
        chain_ids.reshape(1, 64),
        chain_bias.reshape(1, HEADS),
        jnp.transpose(w_bias),
        jnp.transpose(w_attn, (0, 2, 1)),
        w_attn_out,
    )
    return (pair_out.reshape(8, 128, 128), single_out)


def solution(mesh):
    in_specs = (
        P("row", "col", None),
        P("row", "col", None),
        P("row", "col", None),
        P("row", None),
        P("row"),
        P("row"),
        P(),
        P(),
        P(),
        P(),
        P(),
        P(),
        P(None, None, "col"),
        P("col", None),
    )
    out_specs = (P("row", "col", None), P("row", None))
    return jax.shard_map(local, mesh=mesh, in_specs=in_specs, out_specs=out_specs, check_vma=False)
```

```python
import jax
import jax.numpy as jnp
from jax import lax
from jax.experimental import pallas as pl
from jax.experimental.pallas import tpu as pltpu
from jax.sharding import PartitionSpec as P

HEAD_DIM = 24
HEADS = 16
NZ = 8
NY = 4
NQ = 16
GROUP = NY * NQ
SLOT = 32
WIDE = HEADS * SLOT
MESH = pl.DeviceIdType.MESH
EARLY = 48
CHUNK = 16
CHUNKS = 4

epsilon = 1e-05


def layer_norm(values, axis):
    mean_val = jnp.mean(values, axis=axis, keepdims=True)
    centred = values - mean_val
    variance = jnp.mean(centred * centred, axis=axis, keepdims=True)
    return centred * lax.rsqrt(variance + epsilon)


def remote(src, dst, send, recv, row, col):
    return pltpu.make_async_remote_copy(
        src_ref=src, dst_ref=dst, send_sem=send, recv_sem=recv, device_id=(row, col), device_id_type=MESH
    )


def dot(a, b, over_a, over_b):
    return lax.dot_general(a, b, (((over_a,), (over_b,)), ((), ())), preferred_element_type=jnp.float32)


def block_kernel(
    left_any, right_any, pair_any, single_any, w_gate_any, w_out_any, w_in_any, w_down_any, mask_any, chain_any, bias_any, w_bias_any, w_attn_any, w_attn_out_any,
    pair_out, single_out,
    left_in, right_in, lt, rt, lbuf, rbuf, tsend, tin, tin32, gate_tri, kv_msg, kv_all, qg_msg, qg_all, wo_msg, wo_all, proj_in, square,
    q_full, gate_full, bias_all, part, parts, mask_in, chain_in, chain_bias, bias_weights, w_attn, w_attn_out,
    values_low, own_values_kept, own_sum_kept, mask_kept,
    pair, single, w_gate, w_out, w_in, w_down,
    own_sem, in_sem, panel_sem, l_send, l_recv, r_send, r_recv, z_send, z_recv, k_send, k_recv, kz_send, kz_recv,
    q_send, q_recv, w_send, w_recv, t_send, t_recv, p_send, p_recv,
):
    row = lax.axis_index("row")
    col = lax.axis_index("col")
    z = row // NY
    yh = row % NY
    me = yh * NQ + col
    up = lax.rem(z + 1, NZ)
    down = lax.rem(z + NZ - 1, NZ)

    def group_device(m):
        return z * NY + lax.div(m, NQ), lax.rem(m, NQ)

    def others(body, start=1, stop=GROUP):
        def step(n, carry):
            body(lax.rem(me + n, GROUP))
            return carry

        lax.fori_loop(start, stop, step, 0)

    barrier = pltpu.get_barrier_semaphore()

    def greet(m):
        pl.semaphore_signal(barrier, inc=1, device_id=group_device(m), device_id_type=MESH)

    left_copy = pltpu.make_async_copy(left_any, left_in, panel_sem.at[CHUNKS])
    left_copy.start()
    single_copy = pltpu.make_async_copy(single_any, single, own_sem.at[7])
    single_copy.start()

    def right_copy(chunk):
        rows = pl.ds(pl.multiple_of(chunk * CHUNK, CHUNK), CHUNK)
        return pltpu.make_async_copy(right_any.at[rows], right_in.at[rows], panel_sem.at[chunk])

    for chunk in range(CHUNKS):
        right_copy(chunk).start()
    for plane in (up, down):
        pl.semaphore_signal(barrier, inc=1, device_id=(plane * NY + yh, col), device_id_type=MESH)
    for n in range(61, GROUP):
        greet(lax.rem(me + n, GROUP))

    home = lax.div(row, 2)
    k_slot = lax.rem(row, 2) * NQ + col
    k_plane = lax.div(k_slot, 4)

    def k_source(n):
        return 2 * col + lax.div(z, 4), 4 * lax.rem(z, 4) + n

    def k_from_self(n):
        source_row, source_col = k_source(n)
        return (source_row == row) & (source_col == col)

    def k_to_self(n):
        return (k_plane == z) & (n == yh) & (home == col)

    def k_greet(n, carry):
        @pl.when(jnp.logical_not(k_from_self(n)))
        def _():
            pl.semaphore_signal(barrier, inc=1, device_id=k_source(n), device_id_type=MESH)

        return carry

    lax.fori_loop(0, 4, k_greet, 0)

    inputs = [
        pltpu.make_async_copy(source, target, in_sem.at[n])
        for n, (source, target) in enumerate(
            (
                (w_attn_any, w_attn), (mask_any, mask_in), (chain_any, chain_in), (bias_any, chain_bias),
                (w_bias_any, bias_weights), (w_attn_out_any, w_attn_out), (w_gate_any, w_gate), (pair_any, pair),
                (w_out_any, w_out), (w_in_any, w_in), (w_down_any, w_down),
            )
        )
    ]
    for copy in inputs:
        copy.start()

    def l_block(m):
        source_row, source_col = group_device(m)
        return lbuf.at[pl.ds(source_row * 16, 16), pl.ds(source_col * 128, 128)]

    def r_block(m):
        return rbuf.at[m]

    def l_copy(m, slot):
        return remote(lt.at[m], l_block(slot), l_send, l_recv.at[slot], *group_device(m))

    def r_copy(channel, m, slot):
        return remote(
            rt.at[m * 2 + channel], rbuf.at[slot, channel], r_send, r_recv.at[channel, slot],
            *group_device(m),
        )

    def turn(chunk, carry):
        right_copy(chunk).wait()
        for n in range(1, 16):
            if n < 60 // CHUNKS + 1:
                greet(lax.rem(me + chunk * (60 // CHUNKS) + n, GROUP))
        rows = pl.ds(pl.multiple_of(chunk * CHUNK, CHUNK), CHUNK)
        rt[:, rows, :] = jnp.transpose(right_in[rows], (2, 0, 1))
        return carry

    lax.fori_loop(0, CHUNKS, turn, 0)

    l_own = pltpu.make_async_copy(lt.at[me], l_block(me), own_sem.at[0])
    r_own = pltpu.make_async_copy(rt.at[pl.ds(me * 2, 2)], r_block(me), own_sem.at[4])
    r_own.start()

    remaining = k_to_self(yh)
    pl.semaphore_wait(barrier, GROUP + 5 - remaining.astype(jnp.int32))
    others(lambda m: r_copy(0, m, me).start(), 1, 9)
    left_copy.wait()
    lt[...] = jnp.transpose(left_in[...].astype(jnp.float32), (2, 0, 1)).reshape(GROUP, 16, 128).astype(jnp.bfloat16)
    l_own.start()
    others(lambda m: l_copy(m, me).start())
    others(lambda m: r_copy(0, m, me).start(), 9, EARLY)

    proj_in[...] = jnp.zeros_like(proj_in)
    wo_msg[...] = jnp.zeros_like(wo_msg)
    qg_msg[...] = jnp.zeros_like(qg_msg)
    single_copy.wait()
    single_norm = layer_norm(single[...].astype(jnp.float32), -1).astype(jnp.bfloat16)

    for copy in inputs:
        copy.wait()
    for place, which in enumerate((1, 2, 0, 3)):
        proj_in[place * SLOT : place * SLOT + HEAD_DIM, :] = w_attn[which].astype(jnp.float32)
    proj = proj_in[...].astype(jnp.bfloat16)
    key_value = dot(proj[0 : 2 * SLOT], single_norm, 1, 1)
    square[0:SLOT, 0:64] = key_value[0:SLOT]
    square[0:SLOT, 64:128] = key_value[SLOT : 2 * SLOT]
    square[HEAD_DIM : HEAD_DIM + 1, 0:64] = mask_in[...].astype(jnp.float32)
    square[HEAD_DIM : HEAD_DIM + 1, 64:128] = chain_in[...].astype(jnp.float32)
    kv_msg[...] = square[0:SLOT, :].astype(jnp.bfloat16)
    first_rows = dot(single_norm[0:16], proj[2 * SLOT : 4 * SLOT], 1, 1)[0:8]
    scaled = (first_rows * (HEAD_DIM ** (-0.5))).astype(jnp.bfloat16).astype(jnp.float32)
    lane = lax.broadcasted_iota(jnp.int32, (8, 2 * SLOT), 1)
    qg_msg[:, 0 : 2 * SLOT] = jnp.where(lane < SLOT, scaled, jax.nn.sigmoid(first_rows))

    k_own = pltpu.make_async_copy(kv_msg, kv_all.at[k_slot], own_sem.at[1])

    def k_copy(n, slot):
        return remote(kv_msg, kv_all.at[slot], k_send.at[n], k_recv.at[lax.rem(slot, 4)], k_plane * NY + n, home)

    def k_start(n, carry):
        stays = k_to_self(n)

        @pl.when(stays)
        def _():
            k_own.start()

        @pl.when(jnp.logical_not(stays))
        def _():
            k_copy(n, k_slot).start()

        return carry

    lax.fori_loop(0, 4, k_start, 0)

    def q_copy(target, slot):
        return remote(qg_msg, qg_all.at[slot], q_send.at[target], q_recv.at[slot], row, target)

    q_own = pltpu.make_async_copy(qg_msg, qg_all.at[col], own_sem.at[2])
    q_own.start()

    def q_start(n, carry):
        target = lax.rem(col + n, NQ)
        q_copy(target, col).start()
        return carry

    lax.fori_loop(1, NQ, q_start, 0)
    others(lambda m: r_copy(0, m, me).start(), EARLY, GROUP)
    others(lambda m: r_copy(1, m, me).start())

    proj_in[0:SLOT, :] = jnp.zeros((SLOT, 384), jnp.float32)
    proj_in[0:HEAD_DIM, :] = w_attn_out[...].astype(jnp.float32)
    wo_msg[...] = proj_in[0:SLOT, :].astype(jnp.bfloat16)
    square[...] = jnp.zeros_like(square)
    square[:, 0:HEADS] = jnp.broadcast_to(chain_bias[...], (128, HEADS))
    chain_heads = square[...].T[0:HEADS]

    def gates(tile, carry):
        rows = pl.ds(pl.multiple_of(tile * 256, 256), 256)
        pair_norm = layer_norm(pair[rows, :].astype(jnp.float32), -1).astype(jnp.bfloat16)
        gate_tri[rows, :] = jax.nn.sigmoid(dot(pair_norm, w_gate[...], 1, 0))
        return carry

    lax.fori_loop(0, 4, gates, 0)

    l_own.wait()
    others(lambda m: l_copy(m, m).wait_recv())

    def z_copy(plane, way, target_z):
        block = lbuf.at[pl.ds(plane * 64, 64), :]
        return remote(block, block, z_send.at[way, plane], z_recv.at[plane], target_z * NY + yh, col)

    def kz_copy(plane, way, target_z):
        block = kv_all.at[pl.ds(plane * 4, 4)]
        return remote(block, block, kz_send.at[way, plane], kz_recv.at[plane], target_z * NY + yh, col)

    def plane_at(offset):
        return lax.rem(z + NZ + offset, NZ)

    def ring_step(copy, step):
        if step:
            copy(plane_at(-step), 0, up).wait_recv()
        copy(plane_at(-step), 0, up).start()
        if step < 3:
            if step:
                copy(plane_at(step), 1, down).wait_recv()
            copy(plane_at(step), 1, down).start()

    def ring_end(copy):
        copy(plane_at(4), 0, up).wait_recv()
        copy(plane_at(3), 1, down).wait_recv()

    for step in range(4):
        ring_step(z_copy, step)
    ring_end(z_copy)

    def k_wait(n, carry):
        from_self = k_from_self(n)

        @pl.when(from_self)
        def _():
            k_own.wait()

        @pl.when(jnp.logical_not(from_self))
        def _():
            k_copy(0, z * 4 + n).wait_recv()

        return carry

    lax.fori_loop(0, 4, k_wait, 0)

    ring_step(kz_copy, 0)
    r_own.wait()

    def t_copy(channel, m, slot):
        return remote(
            tsend.at[channel, lax.rem(m, 2), lax.div(m, 2)], tin.at[slot, channel],
            t_send, t_recv.at[channel, slot], lax.div(m, 2), 2 * z + lax.rem(m, 2),
        )

    def t_stays(m):
        return (lax.div(m, 2) == row) & (2 * z + lax.rem(m, 2) == col)

    def t_own(channel):
        return pltpu.make_async_copy(tsend.at[channel, col % 2, row], tin.at[me, channel], own_sem.at[5 + channel])

    for channel in range(2):
        others(lambda m: r_copy(channel, m, m).wait_recv())

        def multiply(step, carry):
            tile = lax.rem(step + z, 2)
            rows = pl.ds(pl.multiple_of(tile * 256, 256), 256)
            total = jnp.zeros((256, 256), jnp.float32)
            for pair_of_q in range(NQ // 2):
                right = jnp.concatenate(
                    [
                        jnp.concatenate([rbuf[y * NQ + 2 * pair_of_q + n, channel] for y in range(NY)], axis=0)
                        for n in range(2)
                    ],
                    axis=1,
                )
                total = total + dot(lbuf[rows, pair_of_q * 256 : pair_of_q * 256 + 256], right, 1, 1)
            chosen = total.reshape(16, 2, 8, 256)[:, channel].astype(jnp.bfloat16)
            for half in range(2):
                tsend[channel, half, pl.ds(tile * 16, 16)] = chosen[:, :, half * 128 : half * 128 + 128]

            def t_start(n, inner):
                m = tile * 32 + lax.rem(me + n, 32)
                stays = t_stays(m)

                @pl.when(stays)
                def _():
                    t_own(channel).start()

                @pl.when(jnp.logical_not(stays))
                def _():
                    t_copy(channel, m, me).start()

                return inner

            lax.fori_loop(0, 32, t_start, 0)
            return carry

        lax.fori_loop(0, 2, multiply, 0)
        if channel == 0:
            ring_step(kz_copy, 1)
            q_own.wait()

            def q_wait(n, carry):
                target = lax.rem(col + n, NQ)
                q_copy(target, col).wait_send()
                q_copy(target, target).wait_recv()
                return carry

            lax.fori_loop(1, NQ, q_wait, 0)
            for head in range(HEADS):
                lanes = slice(head * SLOT, head * SLOT + SLOT)
                q_full[:, lanes] = qg_all[head, :, 0:SLOT]
                gate_full[:, lanes] = qg_all[head, :, SLOT : 2 * SLOT]
            ring_step(kz_copy, 2)

    ring_step(kz_copy, 3)
    ring_end(kz_copy)

    low = kv_all[0:HEADS].astype(jnp.float32).reshape(WIDE, 128)
    high = kv_all[HEADS : 2 * HEADS].astype(jnp.float32).reshape(WIDE, 128)
    lane = lax.broadcasted_iota(jnp.int32, (WIDE, 128), 1)
    keys = jnp.where(lane < 64, low, pltpu.roll(high, 64, 1))
    values = jnp.where(lane < 64, pltpu.roll(low, 64, 1), high)
    mask_cols = keys[HEAD_DIM : HEAD_DIM + 1, :]
    chain_cols = values[HEAD_DIM : HEAD_DIM + 1, :]
    head_of_row = lax.broadcasted_iota(jnp.int32, (HEADS, WIDE), 0)
    lane_wide = lax.broadcasted_iota(jnp.int32, (HEADS, WIDE), 1)
    own_block = head_of_row == lax.div(lane_wide, SLOT)
    depth = lax.rem(lane_wide, SLOT)
    own_values = jnp.where(own_block & (depth < HEAD_DIM), 1.0, 0.0)
    own_sum = jnp.where(own_block & (depth == HEAD_DIM), 1.0, 0.0)
    spread = jnp.concatenate(
        [jnp.broadcast_to(q_full[i : i + 1, :], (HEADS, WIDE)) * own_values for i in range(8)], axis=0
    ).astype(jnp.bfloat16)
    same = jnp.concatenate(
        [
            chain_heads * jnp.where(chain_cols == chain_in[0:1, i : i + 1].astype(jnp.float32), 1.0, 0.0)
            for i in range(8)
        ],
        axis=0,
    )
    bias_all[...] = dot(spread, keys.astype(jnp.bfloat16), 1, 0) + same
    values_low[...] = values.astype(jnp.bfloat16)
    own_values_kept[...] = own_values
    own_sum_kept[...] = own_sum
    mask_kept[...] = mask_cols

    for channel in range(2):

        def t_wait(s, carry):
            from_self = (col // 2 == z) & (s == me)

            @pl.when(from_self)
            def _():
                t_own(channel).wait()

            @pl.when(jnp.logical_not(from_self))
            def _():
                t_copy(channel, s, s).wait_recv()

            return carry

        lax.fori_loop(0, GROUP, t_wait, 0)

    tin32[...] = tin[...].astype(jnp.float32).reshape(1024, 128)

    def w_copy(target, slot):
        return remote(wo_msg, wo_all.at[slot], w_send.at[target], w_recv.at[slot], row, target)

    w_own = pltpu.make_async_copy(wo_msg, wo_all.at[col], own_sem.at[3])
    w_own.start()

    hidden = w_down.shape[0]

    def pair_step(step, carry):
        rows = pl.ds(pl.multiple_of(step * 256, 256), 256)
        for n in range(4):
            offset = step * 4 + n

            @pl.when(offset > 0)
            def _():
                w_copy(lax.rem(col + offset, NQ), col).start()

        updates = []
        for inner in range(2):
            block = tin32[pl.ds(step * 2 + inner, 128, stride=8), :]
            updates.append(dot(layer_norm(block, 0).astype(jnp.bfloat16), w_out[...], 0, 0))
        update = jnp.concatenate(updates, axis=0)
        pair_mid = pair[rows, :].astype(jnp.float32) + gate_tri[rows, :] * update
        trans_in = layer_norm(pair_mid, -1).astype(jnp.bfloat16)
        both_parts = dot(trans_in, w_in[...], 1, 0)
        gate_part = both_parts[:, :hidden]
        act = (gate_part / (1.0 + jnp.exp(-gate_part)) * both_parts[:, hidden:]).astype(jnp.bfloat16)
        new_pair = (pair_mid + dot(act, w_down[...], 1, 0)).astype(jnp.bfloat16)
        pair_out[rows, :] = new_pair
        bias_norm = layer_norm(new_pair.astype(jnp.float32), -1).astype(jnp.bfloat16)
        linear = dot(bias_weights[...], bias_norm, 1, 1)
        for inner in range(2):
            place = pl.multiple_of(step * 32 + inner * 16, 16)
            bias_all[pl.ds(place, 16), :] += linear[:, inner * 128 : inner * 128 + 128]
        return carry

    lax.fori_loop(0, 4, pair_step, 0)

    weights = jnp.exp(bias_all[...]) * mask_kept[...]
    denominator = jnp.sum(weights, axis=1, keepdims=True)
    products = dot(weights.astype(jnp.bfloat16), values_low[...], 1, 1)
    for i in range(8):
        span = slice(i * HEADS, i * HEADS + HEADS)
        kept = products[span] * own_values_kept[...] + denominator[span] * own_sum_kept[...]
        part[i : i + 1, :] = jnp.sum(kept, axis=0, keepdims=True)

    def p_copy(target, slot):
        return remote(part, parts.at[slot], p_send.at[target], p_recv.at[slot], row, target)

    def p_start(n, carry):
        p_copy(lax.rem(col + n, NQ), col).start()
        return carry

    lax.fori_loop(1, NQ, p_start, 0)
    p_own = pltpu.make_async_copy(part, parts.at[col], own_sem.at[8])
    p_own.start()

    for step in range(4):
        kz_copy(plane_at(-step), 0, up).wait_send()
        if step < 3:
            kz_copy(plane_at(step), 1, down).wait_send()

    def sent(ref, sem):
        remote(ref, ref, sem, own_sem.at[9], up * NY + yh, col).wait_send()

    sent(lt.at[pl.ds(0, GROUP - 1)], l_send)
    sent(rt.at[pl.ds(0, 2 * GROUP - 2)], r_send)
    keeps_one = lax.div(col, 2) == z

    @pl.when(keeps_one)
    def _():
        sent(tin.at[pl.ds(0, GROUP - 1)], t_send)

    @pl.when(jnp.logical_not(keeps_one))
    def _():
        sent(tin, t_send)

    for step in range(4):
        z_copy(plane_at(-step), 0, up).wait_send()
        if step < 3:
            z_copy(plane_at(step), 1, down).wait_send()

    def k_sent(n, carry):
        @pl.when(jnp.logical_not(k_to_self(n)))
        def _():
            k_copy(n, k_slot).wait_send()

        return carry

    lax.fori_loop(0, 4, k_sent, 0)

    w_own.wait()

    def w_wait(n, carry):
        target = lax.rem(col + n, NQ)
        w_copy(target, target).wait_recv()
        w_copy(target, col).wait_send()
        return carry

    lax.fori_loop(1, NQ, w_wait, 0)
    out_weights = wo_all[...].reshape(WIDE, 384)
    p_own.wait()

    def p_wait(n, carry):
        target = lax.rem(col + n, NQ)
        p_copy(target, target).wait_recv()
        p_copy(target, col).wait_send()
        return carry

    lax.fori_loop(1, NQ, p_wait, 0)
    total = parts[0]
    for n in range(1, NQ):
        total = total + parts[n]
    lane = lax.rem(lax.broadcasted_iota(jnp.int32, (8, WIDE), 1), SLOT)
    below = jnp.where(lane == HEAD_DIM, total, 0.0)
    for shift in (1, 2, 4, 8, 16):
        below = below + pltpu.roll(below, WIDE - shift, 1)
    gated = (gate_full[...] * (total / below)).astype(jnp.bfloat16)
    mixed = dot(gated, out_weights, 1, 0)
    single_out[...] = (single[0:8, :].astype(jnp.float32) + mixed).astype(jnp.bfloat16)


def block(*operands):
    dma = pltpu.SemaphoreType.DMA
    vmem = pl.BlockSpec(memory_space=pltpu.VMEM)
    anywhere = pl.BlockSpec(memory_space=pltpu.HBM)
    return pl.pallas_call(
        block_kernel,
        out_shape=(
            pltpu.VMEM((1024, 128), jnp.bfloat16),
            pltpu.VMEM((8, 384), jnp.bfloat16),
        ),
        in_specs=[anywhere] * 14,
        out_specs=(vmem, vmem),
        scratch_shapes=[
            pltpu.VMEM((8, 128, 128), jnp.bfloat16),
            pltpu.VMEM((64, 128, 128), jnp.bfloat16),
            pltpu.VMEM((GROUP, 16, 128), jnp.bfloat16),
            pltpu.VMEM((128, 64, 128), jnp.bfloat16),
            pltpu.VMEM((512, 2048), jnp.bfloat16),
            pltpu.VMEM((GROUP, 2, 64, 128), jnp.bfloat16),
            pltpu.VMEM((2, 2, 32, 8, 128), jnp.bfloat16),
            pltpu.VMEM((GROUP, 2, 8, 128), jnp.bfloat16),
            pltpu.VMEM((1024, 128), jnp.float32),
            pltpu.VMEM((1024, 128), jnp.float32),
            pltpu.VMEM((SLOT, 128), jnp.bfloat16),
            pltpu.VMEM((2 * NQ, SLOT, 128), jnp.bfloat16),
            pltpu.VMEM((8, 128), jnp.float32),
            pltpu.VMEM((NQ, 8, 128), jnp.float32),
            pltpu.VMEM((SLOT, 384), jnp.bfloat16),
            pltpu.VMEM((NQ, SLOT, 384), jnp.bfloat16),
            pltpu.VMEM((128, 384), jnp.float32),
            pltpu.VMEM((128, 128), jnp.float32),
            pltpu.VMEM((8, WIDE), jnp.float32),
            pltpu.VMEM((8, WIDE), jnp.float32),
            pltpu.VMEM((128, 128), jnp.float32),
            pltpu.VMEM((8, WIDE), jnp.float32),
            pltpu.VMEM((NQ, 8, WIDE), jnp.float32),
            pltpu.VMEM((1, 64), jnp.int32),
            pltpu.VMEM((1, 64), jnp.int32),
            pltpu.VMEM((1, HEADS), jnp.float32),
            pltpu.VMEM((HEADS, 128), jnp.bfloat16),
            pltpu.VMEM((4, HEAD_DIM, 384), jnp.bfloat16),
            pltpu.VMEM((HEAD_DIM, 384), jnp.bfloat16),
            pltpu.VMEM((WIDE, 128), jnp.bfloat16),
            pltpu.VMEM((HEADS, WIDE), jnp.float32),
            pltpu.VMEM((HEADS, WIDE), jnp.float32),
            pltpu.VMEM((1, 128), jnp.float32),
            pltpu.VMEM((1024, 128), jnp.bfloat16),
            pltpu.VMEM((64, 384), jnp.bfloat16),
            pltpu.VMEM((128, 128), jnp.bfloat16),
            pltpu.VMEM((128, 128), jnp.bfloat16),
            pltpu.VMEM((128, 1024), jnp.bfloat16),
            pltpu.VMEM((512, 128), jnp.bfloat16),
            dma((10,)),
            dma((11,)),
            dma((CHUNKS + 1,)),
            dma,
            dma((GROUP,)),
            dma,
            dma((2, GROUP)),
            dma((2, NZ)),
            dma((NZ,)),
            dma((4,)),
            dma((4,)),
            dma((2, NZ)),
            dma((NZ,)),
            dma((NQ,)),
            dma((NQ,)),
            dma((NQ,)),
            dma((NQ,)),
            dma,
            dma((2, GROUP)),
            dma((NQ,)),
            dma((NQ,)),
        ],
        compiler_params=pltpu.CompilerParams(
            collective_id=0, has_side_effects=True, vmem_limit_bytes=58 * 1024 * 1024
        ),
        name="pairformer",
    )(*operands)


def local(
    pair,
    panel_left,
    panel_right,
    single,
    token_mask,
    chain_ids,
    w_tri_gate,
    w_tri_out,
    w_trans_in,
    w_trans_down,
    w_bias,
    chain_bias,
    w_attn,
    w_attn_out,
):
    pair_out, single_out = block(
        panel_left,
        panel_right,
        pair.reshape(1024, 128),
        single,
        w_tri_gate,
        w_tri_out,
        w_trans_in,
        w_trans_down,
        token_mask.reshape(1, 64),
        chain_ids.reshape(1, 64),
        chain_bias.reshape(1, HEADS),
        jnp.transpose(w_bias),
        jnp.transpose(w_attn, (0, 2, 1)),
        w_attn_out,
    )
    return (pair_out.reshape(8, 128, 128), single_out)


def solution(mesh):
    in_specs = (
        P("row", "col", None),
        P("row", "col", None),
        P("row", "col", None),
        P("row", None),
        P("row"),
        P("row"),
        P(),
        P(),
        P(),
        P(),
        P(),
        P(),
        P(None, None, "col"),
        P("col", None),
    )
    out_specs = (P("row", "col", None), P("row", None))
    return jax.shard_map(local, mesh=mesh, in_specs=in_specs, out_specs=out_specs, check_vma=False)
```

```python
import jax
import jax.numpy as jnp
from jax import lax
from jax.experimental import pallas as pl
from jax.experimental.pallas import tpu as pltpu
from jax.sharding import PartitionSpec as P

HEAD_DIM = 24
HEADS = 16
NZ = 8
NY = 4
NQ = 16
GROUP = NY * NQ
SLOT = 32
WIDE = HEADS * SLOT
MESH = pl.DeviceIdType.MESH
EARLY = 48
CHUNK = 16
CHUNKS = 4

epsilon = 1e-05


def layer_norm(values, axis):
    mean_val = jnp.mean(values, axis=axis, keepdims=True)
    centred = values - mean_val
    variance = jnp.mean(centred * centred, axis=axis, keepdims=True)
    return centred * lax.rsqrt(variance + epsilon)


def remote(src, dst, send, recv, row, col):
    return pltpu.make_async_remote_copy(
        src_ref=src, dst_ref=dst, send_sem=send, recv_sem=recv, device_id=(row, col), device_id_type=MESH
    )


def dot(a, b, over_a, over_b):
    return lax.dot_general(a, b, (((over_a,), (over_b,)), ((), ())), preferred_element_type=jnp.float32)


def block_kernel(
    left_any, right_any, pair_any, single_any, w_gate_any, w_out_any, w_in_any, w_down_any, mask_any, chain_any, bias_any, w_bias_any, w_attn_any, w_attn_out_any,
    pair_out, single_out,
    left_in, right_in, lt, rt, lbuf, rbuf, tsend, tin, tin32, gate_tri, kv_msg, kv_all, qg_msg, qg_all, wo_msg, wo_all, proj_in, square,
    q_full, gate_full, bias_all, part, parts, mask_in, chain_in, chain_bias, bias_weights, w_attn, w_attn_out,
    values_low, own_values_kept, own_sum_kept, mask_kept,
    pair, single, w_gate, w_out, w_in, w_down,
    own_sem, in_sem, panel_sem, l_send, l_recv, r_send, r_recv, z_send, z_recv, k_send, k_recv, kz_send, kz_recv,
    q_send, q_recv, w_send, w_recv, t_send, t_recv, p_send, p_recv,
):
    row = lax.axis_index("row")
    col = lax.axis_index("col")
    z = row // NY
    yh = row % NY
    me = yh * NQ + col
    up = lax.rem(z + 1, NZ)
    down = lax.rem(z + NZ - 1, NZ)

    def group_device(m):
        return z * NY + lax.div(m, NQ), lax.rem(m, NQ)

    def others(body, start=1, stop=GROUP):
        def step(n, carry):
            body(lax.rem(me + n, GROUP))
            return carry

        lax.fori_loop(start, stop, step, 0)

    barrier = pltpu.get_barrier_semaphore()

    def greet(m):
        pl.semaphore_signal(barrier, inc=1, device_id=group_device(m), device_id_type=MESH)

    left_copy = pltpu.make_async_copy(left_any, left_in, panel_sem.at[CHUNKS])
    left_copy.start()
    single_copy = pltpu.make_async_copy(single_any, single, own_sem.at[7])
    single_copy.start()

    def right_copy(chunk):
        rows = pl.ds(pl.multiple_of(chunk * CHUNK, CHUNK), CHUNK)
        return pltpu.make_async_copy(right_any.at[rows], right_in.at[rows], panel_sem.at[chunk])

    for chunk in range(CHUNKS):
        right_copy(chunk).start()
    for plane in (up, down):
        pl.semaphore_signal(barrier, inc=1, device_id=(plane * NY + yh, col), device_id_type=MESH)
    for n in range(61, GROUP):
        greet(lax.rem(me + n, GROUP))

    home = lax.div(row, 2)
    k_slot = lax.rem(row, 2) * NQ + col
    k_plane = lax.div(k_slot, 4)

    def k_source(n):
        return 2 * col + lax.div(z, 4), 4 * lax.rem(z, 4) + n

    def k_from_self(n):
        source_row, source_col = k_source(n)
        return (source_row == row) & (source_col == col)

    def k_to_self(n):
        return (k_plane == z) & (n == yh) & (home == col)

    def k_greet(n, carry):
        @pl.when(jnp.logical_not(k_from_self(n)))
        def _():
            pl.semaphore_signal(barrier, inc=1, device_id=k_source(n), device_id_type=MESH)

        return carry

    lax.fori_loop(0, 4, k_greet, 0)

    inputs = [
        pltpu.make_async_copy(source, target, in_sem.at[n])
        for n, (source, target) in enumerate(
            (
                (w_attn_any, w_attn), (mask_any, mask_in), (chain_any, chain_in), (bias_any, chain_bias),
                (w_bias_any, bias_weights), (w_attn_out_any, w_attn_out), (w_gate_any, w_gate), (pair_any, pair),
                (w_out_any, w_out), (w_in_any, w_in), (w_down_any, w_down),
            )
        )
    ]
    for copy in inputs:
        copy.start()

    def l_block(m):
        source_row, source_col = group_device(m)
        return lbuf.at[pl.ds(source_row * 16, 16), pl.ds(source_col * 128, 128)]

    def r_block(m):
        return rbuf.at[m]

    def l_copy(m, slot):
        return remote(lt.at[m], l_block(slot), l_send, l_recv.at[slot], *group_device(m))

    def r_copy(channel, m, slot):
        return remote(
            rt.at[m * 2 + channel], rbuf.at[slot, channel], r_send, r_recv.at[channel, slot],
            *group_device(m),
        )

    def turn(chunk, carry):
        right_copy(chunk).wait()
        for n in range(1, 16):
            if n < 60 // CHUNKS + 1:
                greet(lax.rem(me + chunk * (60 // CHUNKS) + n, GROUP))
        rows = pl.ds(pl.multiple_of(chunk * CHUNK, CHUNK), CHUNK)
        rt[:, rows, :] = jnp.transpose(right_in[rows], (2, 0, 1))
        return carry

    lax.fori_loop(0, CHUNKS, turn, 0)

    l_own = pltpu.make_async_copy(lt.at[me], l_block(me), own_sem.at[0])
    r_own = pltpu.make_async_copy(rt.at[pl.ds(me * 2, 2)], r_block(me), own_sem.at[4])
    r_own.start()

    remaining = k_to_self(yh)
    pl.semaphore_wait(barrier, GROUP + 5 - remaining.astype(jnp.int32))
    others(lambda m: r_copy(0, m, me).start(), 1, 4)
    left_copy.wait()
    lt[...] = jnp.transpose(left_in[...].astype(jnp.float32), (2, 0, 1)).reshape(GROUP, 16, 128).astype(jnp.bfloat16)
    l_own.start()
    others(lambda m: l_copy(m, me).start())
    others(lambda m: r_copy(0, m, me).start(), 4, EARLY)

    proj_in[...] = jnp.zeros_like(proj_in)
    wo_msg[...] = jnp.zeros_like(wo_msg)
    qg_msg[...] = jnp.zeros_like(qg_msg)
    single_copy.wait()
    single_norm = layer_norm(single[...].astype(jnp.float32), -1).astype(jnp.bfloat16)

    for copy in inputs:
        copy.wait()
    for place, which in enumerate((1, 2, 0, 3)):
        proj_in[place * SLOT : place * SLOT + HEAD_DIM, :] = w_attn[which].astype(jnp.float32)
    proj = proj_in[...].astype(jnp.bfloat16)
    key_value = dot(proj[0 : 2 * SLOT], single_norm, 1, 1)
    square[0:SLOT, 0:64] = key_value[0:SLOT]
    square[0:SLOT, 64:128] = key_value[SLOT : 2 * SLOT]
    square[HEAD_DIM : HEAD_DIM + 1, 0:64] = mask_in[...].astype(jnp.float32)
    square[HEAD_DIM : HEAD_DIM + 1, 64:128] = chain_in[...].astype(jnp.float32)
    kv_msg[...] = square[0:SLOT, :].astype(jnp.bfloat16)
    first_rows = dot(single_norm[0:16], proj[2 * SLOT : 4 * SLOT], 1, 1)[0:8]
    scaled = (first_rows * (HEAD_DIM ** (-0.5))).astype(jnp.bfloat16).astype(jnp.float32)
    lane = lax.broadcasted_iota(jnp.int32, (8, 2 * SLOT), 1)
    qg_msg[:, 0 : 2 * SLOT] = jnp.where(lane < SLOT, scaled, jax.nn.sigmoid(first_rows))

    k_own = pltpu.make_async_copy(kv_msg, kv_all.at[k_slot], own_sem.at[1])

    def k_copy(n, slot):
        return remote(kv_msg, kv_all.at[slot], k_send.at[n], k_recv.at[lax.rem(slot, 4)], k_plane * NY + n, home)

    def k_start(n, carry):
        stays = k_to_self(n)

        @pl.when(stays)
        def _():
            k_own.start()

        @pl.when(jnp.logical_not(stays))
        def _():
            k_copy(n, k_slot).start()

        return carry

    lax.fori_loop(0, 4, k_start, 0)

    def q_copy(target, slot):
        return remote(qg_msg, qg_all.at[slot], q_send.at[target], q_recv.at[slot], row, target)

    q_own = pltpu.make_async_copy(qg_msg, qg_all.at[col], own_sem.at[2])
    q_own.start()

    def q_start(n, carry):
        target = lax.rem(col + n, NQ)
        q_copy(target, col).start()
        return carry

    lax.fori_loop(1, NQ, q_start, 0)
    others(lambda m: r_copy(0, m, me).start(), EARLY, GROUP)
    others(lambda m: r_copy(1, m, me).start())

    proj_in[0:SLOT, :] = jnp.zeros((SLOT, 384), jnp.float32)
    proj_in[0:HEAD_DIM, :] = w_attn_out[...].astype(jnp.float32)
    wo_msg[...] = proj_in[0:SLOT, :].astype(jnp.bfloat16)
    square[...] = jnp.zeros_like(square)
    square[:, 0:HEADS] = jnp.broadcast_to(chain_bias[...], (128, HEADS))
    chain_heads = square[...].T[0:HEADS]

    def gates(tile, carry):
        rows = pl.ds(pl.multiple_of(tile * 256, 256), 256)
        pair_norm = layer_norm(pair[rows, :].astype(jnp.float32), -1).astype(jnp.bfloat16)
        gate_tri[rows, :] = jax.nn.sigmoid(dot(pair_norm, w_gate[...], 1, 0))
        return carry

    lax.fori_loop(0, 4, gates, 0)

    l_own.wait()
    others(lambda m: l_copy(m, m).wait_recv())

    def z_copy(plane, way, target_z):
        block = lbuf.at[pl.ds(plane * 64, 64), :]
        return remote(block, block, z_send.at[way, plane], z_recv.at[plane], target_z * NY + yh, col)

    def kz_copy(plane, way, target_z):
        block = kv_all.at[pl.ds(plane * 4, 4)]
        return remote(block, block, kz_send.at[way, plane], kz_recv.at[plane], target_z * NY + yh, col)

    def plane_at(offset):
        return lax.rem(z + NZ + offset, NZ)

    def ring_step(copy, step):
        if step:
            copy(plane_at(-step), 0, up).wait_recv()
        copy(plane_at(-step), 0, up).start()
        if step < 3:
            if step:
                copy(plane_at(step), 1, down).wait_recv()
            copy(plane_at(step), 1, down).start()

    def ring_end(copy):
        copy(plane_at(4), 0, up).wait_recv()
        copy(plane_at(3), 1, down).wait_recv()

    for step in range(4):
        ring_step(z_copy, step)
    ring_end(z_copy)

    def k_wait(n, carry):
        from_self = k_from_self(n)

        @pl.when(from_self)
        def _():
            k_own.wait()

        @pl.when(jnp.logical_not(from_self))
        def _():
            k_copy(0, z * 4 + n).wait_recv()

        return carry

    lax.fori_loop(0, 4, k_wait, 0)

    ring_step(kz_copy, 0)
    r_own.wait()

    def t_copy(channel, m, slot):
        return remote(
            tsend.at[channel, lax.rem(m, 2), lax.div(m, 2)], tin.at[slot, channel],
            t_send, t_recv.at[channel, slot], lax.div(m, 2), 2 * z + lax.rem(m, 2),
        )

    def t_stays(m):
        return (lax.div(m, 2) == row) & (2 * z + lax.rem(m, 2) == col)

    def t_own(channel):
        return pltpu.make_async_copy(tsend.at[channel, col % 2, row], tin.at[me, channel], own_sem.at[5 + channel])

    for channel in range(2):
        others(lambda m: r_copy(channel, m, m).wait_recv())

        def multiply(step, carry):
            tile = lax.rem(step + z, 2)
            rows = pl.ds(pl.multiple_of(tile * 256, 256), 256)
            total = jnp.zeros((256, 256), jnp.float32)
            for pair_of_q in range(NQ // 2):
                right = jnp.concatenate(
                    [
                        jnp.concatenate([rbuf[y * NQ + 2 * pair_of_q + n, channel] for y in range(NY)], axis=0)
                        for n in range(2)
                    ],
                    axis=1,
                )
                total = total + dot(lbuf[rows, pair_of_q * 256 : pair_of_q * 256 + 256], right, 1, 1)
            chosen = total.reshape(16, 2, 8, 256)[:, channel].astype(jnp.bfloat16)
            for half in range(2):
                tsend[channel, half, pl.ds(tile * 16, 16)] = chosen[:, :, half * 128 : half * 128 + 128]

            def t_start(n, inner):
                m = tile * 32 + lax.rem(me + n, 32)
                stays = t_stays(m)

                @pl.when(stays)
                def _():
                    t_own(channel).start()

                @pl.when(jnp.logical_not(stays))
                def _():
                    t_copy(channel, m, me).start()

                return inner

            lax.fori_loop(0, 32, t_start, 0)
            return carry

        lax.fori_loop(0, 2, multiply, 0)
        if channel == 0:
            ring_step(kz_copy, 1)
            ring_step(kz_copy, 2)

    ring_step(kz_copy, 3)
    q_own.wait()

    def q_wait(n, carry):
        target = lax.rem(col + n, NQ)
        q_copy(target, col).wait_send()
        q_copy(target, target).wait_recv()
        return carry

    lax.fori_loop(1, NQ, q_wait, 0)
    for head in range(HEADS):
        lanes = slice(head * SLOT, head * SLOT + SLOT)
        q_full[:, lanes] = qg_all[head, :, 0:SLOT]
        gate_full[:, lanes] = qg_all[head, :, SLOT : 2 * SLOT]
    ring_end(kz_copy)

    low = kv_all[0:HEADS].astype(jnp.float32).reshape(WIDE, 128)
    high = kv_all[HEADS : 2 * HEADS].astype(jnp.float32).reshape(WIDE, 128)
    lane = lax.broadcasted_iota(jnp.int32, (WIDE, 128), 1)
    keys = jnp.where(lane < 64, low, pltpu.roll(high, 64, 1))
    values = jnp.where(lane < 64, pltpu.roll(low, 64, 1), high)
    mask_cols = keys[HEAD_DIM : HEAD_DIM + 1, :]
    chain_cols = values[HEAD_DIM : HEAD_DIM + 1, :]
    head_of_row = lax.broadcasted_iota(jnp.int32, (HEADS, WIDE), 0)
    lane_wide = lax.broadcasted_iota(jnp.int32, (HEADS, WIDE), 1)
    own_block = head_of_row == lax.div(lane_wide, SLOT)
    depth = lax.rem(lane_wide, SLOT)
    own_values = jnp.where(own_block & (depth < HEAD_DIM), 1.0, 0.0)
    own_sum = jnp.where(own_block & (depth == HEAD_DIM), 1.0, 0.0)
    spread = jnp.concatenate(
        [jnp.broadcast_to(q_full[i : i + 1, :], (HEADS, WIDE)) * own_values for i in range(8)], axis=0
    ).astype(jnp.bfloat16)
    same = jnp.concatenate(
        [
            chain_heads * jnp.where(chain_cols == chain_in[0:1, i : i + 1].astype(jnp.float32), 1.0, 0.0)
            for i in range(8)
        ],
        axis=0,
    )
    bias_all[...] = dot(spread, keys.astype(jnp.bfloat16), 1, 0) + same
    values_low[...] = values.astype(jnp.bfloat16)
    own_values_kept[...] = own_values
    own_sum_kept[...] = own_sum
    mask_kept[...] = mask_cols

    for channel in range(2):

        def t_wait(s, carry):
            from_self = (col // 2 == z) & (s == me)

            @pl.when(from_self)
            def _():
                t_own(channel).wait()

            @pl.when(jnp.logical_not(from_self))
            def _():
                t_copy(channel, s, s).wait_recv()

            return carry

        lax.fori_loop(0, GROUP, t_wait, 0)

    tin32[...] = tin[...].astype(jnp.float32).reshape(1024, 128)

    def w_copy(target, slot):
        return remote(wo_msg, wo_all.at[slot], w_send.at[target], w_recv.at[slot], row, target)

    w_own = pltpu.make_async_copy(wo_msg, wo_all.at[col], own_sem.at[3])
    w_own.start()

    hidden = w_down.shape[0]

    def pair_step(step, carry):
        rows = pl.ds(pl.multiple_of(step * 256, 256), 256)
        for n in range(4):
            offset = step * 4 + n

            @pl.when(offset > 0)
            def _():
                w_copy(lax.rem(col + offset, NQ), col).start()

        updates = []
        for inner in range(2):
            block = tin32[pl.ds(step * 2 + inner, 128, stride=8), :]
            updates.append(dot(layer_norm(block, 0).astype(jnp.bfloat16), w_out[...], 0, 0))
        update = jnp.concatenate(updates, axis=0)
        pair_mid = pair[rows, :].astype(jnp.float32) + gate_tri[rows, :] * update
        trans_in = layer_norm(pair_mid, -1).astype(jnp.bfloat16)
        both_parts = dot(trans_in, w_in[...], 1, 0)
        gate_part = both_parts[:, :hidden]
        act = (gate_part / (1.0 + jnp.exp(-gate_part)) * both_parts[:, hidden:]).astype(jnp.bfloat16)
        new_pair = (pair_mid + dot(act, w_down[...], 1, 0)).astype(jnp.bfloat16)
        pair_out[rows, :] = new_pair
        bias_norm = layer_norm(new_pair.astype(jnp.float32), -1).astype(jnp.bfloat16)
        linear = dot(bias_weights[...], bias_norm, 1, 1)
        for inner in range(2):
            place = pl.multiple_of(step * 32 + inner * 16, 16)
            bias_all[pl.ds(place, 16), :] += linear[:, inner * 128 : inner * 128 + 128]
        return carry

    lax.fori_loop(0, 4, pair_step, 0)

    weights = jnp.exp(bias_all[...]) * mask_kept[...]
    denominator = jnp.sum(weights, axis=1, keepdims=True)
    products = dot(weights.astype(jnp.bfloat16), values_low[...], 1, 1)
    for i in range(8):
        span = slice(i * HEADS, i * HEADS + HEADS)
        kept = products[span] * own_values_kept[...] + denominator[span] * own_sum_kept[...]
        part[i : i + 1, :] = jnp.sum(kept, axis=0, keepdims=True)

    def p_copy(target, slot):
        return remote(part, parts.at[slot], p_send.at[target], p_recv.at[slot], row, target)

    def p_start(n, carry):
        p_copy(lax.rem(col + n, NQ), col).start()
        return carry

    lax.fori_loop(1, NQ, p_start, 0)
    p_own = pltpu.make_async_copy(part, parts.at[col], own_sem.at[8])
    p_own.start()

    for step in range(4):
        kz_copy(plane_at(-step), 0, up).wait_send()
        if step < 3:
            kz_copy(plane_at(step), 1, down).wait_send()

    def sent(ref, sem):
        remote(ref, ref, sem, own_sem.at[9], up * NY + yh, col).wait_send()

    sent(lt.at[pl.ds(0, GROUP - 1)], l_send)
    sent(rt.at[pl.ds(0, 2 * GROUP - 2)], r_send)
    keeps_one = lax.div(col, 2) == z

    @pl.when(keeps_one)
    def _():
        sent(tin.at[pl.ds(0, GROUP - 1)], t_send)

    @pl.when(jnp.logical_not(keeps_one))
    def _():
        sent(tin, t_send)

    for step in range(4):
        z_copy(plane_at(-step), 0, up).wait_send()
        if step < 3:
            z_copy(plane_at(step), 1, down).wait_send()

    def k_sent(n, carry):
        @pl.when(jnp.logical_not(k_to_self(n)))
        def _():
            k_copy(n, k_slot).wait_send()

        return carry

    lax.fori_loop(0, 4, k_sent, 0)

    w_own.wait()

    def w_wait(n, carry):
        target = lax.rem(col + n, NQ)
        w_copy(target, target).wait_recv()
        w_copy(target, col).wait_send()
        return carry

    lax.fori_loop(1, NQ, w_wait, 0)
    out_weights = wo_all[...].reshape(WIDE, 384)
    p_own.wait()

    def p_wait(n, carry):
        target = lax.rem(col + n, NQ)
        p_copy(target, target).wait_recv()
        p_copy(target, col).wait_send()
        return carry

    lax.fori_loop(1, NQ, p_wait, 0)
    total = parts[0]
    for n in range(1, NQ):
        total = total + parts[n]
    lane = lax.rem(lax.broadcasted_iota(jnp.int32, (8, WIDE), 1), SLOT)
    below = jnp.where(lane == HEAD_DIM, total, 0.0)
    for shift in (1, 2, 4, 8, 16):
        below = below + pltpu.roll(below, WIDE - shift, 1)
    gated = (gate_full[...] * (total / below)).astype(jnp.bfloat16)
    mixed = dot(gated, out_weights, 1, 0)
    single_out[...] = (single[0:8, :].astype(jnp.float32) + mixed).astype(jnp.bfloat16)


def block(*operands):
    dma = pltpu.SemaphoreType.DMA
    vmem = pl.BlockSpec(memory_space=pltpu.VMEM)
    anywhere = pl.BlockSpec(memory_space=pltpu.HBM)
    return pl.pallas_call(
        block_kernel,
        out_shape=(
            pltpu.VMEM((1024, 128), jnp.bfloat16),
            pltpu.VMEM((8, 384), jnp.bfloat16),
        ),
        in_specs=[anywhere] * 14,
        out_specs=(vmem, vmem),
        scratch_shapes=[
            pltpu.VMEM((8, 128, 128), jnp.bfloat16),
            pltpu.VMEM((64, 128, 128), jnp.bfloat16),
            pltpu.VMEM((GROUP, 16, 128), jnp.bfloat16),
            pltpu.VMEM((128, 64, 128), jnp.bfloat16),
            pltpu.VMEM((512, 2048), jnp.bfloat16),
            pltpu.VMEM((GROUP, 2, 64, 128), jnp.bfloat16),
            pltpu.VMEM((2, 2, 32, 8, 128), jnp.bfloat16),
            pltpu.VMEM((GROUP, 2, 8, 128), jnp.bfloat16),
            pltpu.VMEM((1024, 128), jnp.float32),
            pltpu.VMEM((1024, 128), jnp.float32),
            pltpu.VMEM((SLOT, 128), jnp.bfloat16),
            pltpu.VMEM((2 * NQ, SLOT, 128), jnp.bfloat16),
            pltpu.VMEM((8, 128), jnp.float32),
            pltpu.VMEM((NQ, 8, 128), jnp.float32),
            pltpu.VMEM((SLOT, 384), jnp.bfloat16),
            pltpu.VMEM((NQ, SLOT, 384), jnp.bfloat16),
            pltpu.VMEM((128, 384), jnp.float32),
            pltpu.VMEM((128, 128), jnp.float32),
            pltpu.VMEM((8, WIDE), jnp.float32),
            pltpu.VMEM((8, WIDE), jnp.float32),
            pltpu.VMEM((128, 128), jnp.float32),
            pltpu.VMEM((8, WIDE), jnp.float32),
            pltpu.VMEM((NQ, 8, WIDE), jnp.float32),
            pltpu.VMEM((1, 64), jnp.int32),
            pltpu.VMEM((1, 64), jnp.int32),
            pltpu.VMEM((1, HEADS), jnp.float32),
            pltpu.VMEM((HEADS, 128), jnp.bfloat16),
            pltpu.VMEM((4, HEAD_DIM, 384), jnp.bfloat16),
            pltpu.VMEM((HEAD_DIM, 384), jnp.bfloat16),
            pltpu.VMEM((WIDE, 128), jnp.bfloat16),
            pltpu.VMEM((HEADS, WIDE), jnp.float32),
            pltpu.VMEM((HEADS, WIDE), jnp.float32),
            pltpu.VMEM((1, 128), jnp.float32),
            pltpu.VMEM((1024, 128), jnp.bfloat16),
            pltpu.VMEM((64, 384), jnp.bfloat16),
            pltpu.VMEM((128, 128), jnp.bfloat16),
            pltpu.VMEM((128, 128), jnp.bfloat16),
            pltpu.VMEM((128, 1024), jnp.bfloat16),
            pltpu.VMEM((512, 128), jnp.bfloat16),
            dma((10,)),
            dma((11,)),
            dma((CHUNKS + 1,)),
            dma,
            dma((GROUP,)),
            dma,
            dma((2, GROUP)),
            dma((2, NZ)),
            dma((NZ,)),
            dma((4,)),
            dma((4,)),
            dma((2, NZ)),
            dma((NZ,)),
            dma((NQ,)),
            dma((NQ,)),
            dma((NQ,)),
            dma((NQ,)),
            dma,
            dma((2, GROUP)),
            dma((NQ,)),
            dma((NQ,)),
        ],
        compiler_params=pltpu.CompilerParams(
            collective_id=0, has_side_effects=True, vmem_limit_bytes=58 * 1024 * 1024
        ),
        name="pairformer",
    )(*operands)


def local(
    pair,
    panel_left,
    panel_right,
    single,
    token_mask,
    chain_ids,
    w_tri_gate,
    w_tri_out,
    w_trans_in,
    w_trans_down,
    w_bias,
    chain_bias,
    w_attn,
    w_attn_out,
):
    pair_out, single_out = block(
        panel_left,
        panel_right,
        pair.reshape(1024, 128),
        single,
        w_tri_gate,
        w_tri_out,
        w_trans_in,
        w_trans_down,
        token_mask.reshape(1, 64),
        chain_ids.reshape(1, 64),
        chain_bias.reshape(1, HEADS),
        jnp.transpose(w_bias),
        jnp.transpose(w_attn, (0, 2, 1)),
        w_attn_out,
    )
    return (pair_out.reshape(8, 128, 128), single_out)


def solution(mesh):
    in_specs = (
        P("row", "col", None),
        P("row", "col", None),
        P("row", "col", None),
        P("row", None),
        P("row"),
        P("row"),
        P(),
        P(),
        P(),
        P(),
        P(),
        P(),
        P(None, None, "col"),
        P("col", None),
    )
    out_specs = (P("row", "col", None), P("row", None))
    return jax.shard_map(local, mesh=mesh, in_specs=in_specs, out_specs=out_specs, check_vma=False)
```
